128 devices in a mesh: dp: 16 (over y_lo, z, core), ctx: 8 (over y_hi, x).
Axes of the slice: x: 4, y: 4 (y_hi: 2, y_lo: 2; y = y_hi * 2 + y_lo), z: 4, core: 2. Of those that a mesh axis runs over, the one named last changes fastest.
Arguments:
- inputs: bfloat16 [32, 1024, 1024], P('dp', 'ctx'), may hold values from -6 to 6
- positions: int32 [32, 1024], P('dp'), may hold values from 0 to 1023, as said below
- first_gain: float32 [1024], replicated, may hold values from 0.5 to 1.5
- first_shift: float32 [1024], replicated, may hold values from -4 to 4
- second_gain: float32 [1024], replicated, may hold values from 0.5 to 1.5
- second_shift: float32 [1024], replicated, may hold values from -4 to 4
- project_weight: bfloat16 [1024, 3072], P(('dp', 'ctx')), may hold values from -0.1875 to 0.1875
- project_bias: float32 [3072], replicated, may hold values from -4 to 4
- output_weight: bfloat16 [1024, 1024], P(('dp', 'ctx')), may hold values from -2 to 2
- output_bias: float32 [1024], replicated, may hold values from -4 to 4
- expand_weight: bfloat16 [1024, 4096], P(('dp', 'ctx')), may hold values from -0.1875 to 0.1875
- expand_bias: float32 [4096], replicated, may hold values from -4 to 4
- reduce_weight: bfloat16 [1024, 4, 1024], P(('dp', 'ctx')), may hold values from -0.09375 to 0.09375
- reduce_bias: float32 [1024], replicated, may hold values from -4 to 4
- cotangent: bfloat16 [32, 1024, 1024], P('dp', 'ctx'), may hold values from -6 to 6
Outputs:
- block_output: bfloat16 [32, 1024, 1024], P('dp', 'ctx')
- inputs_grad: bfloat16 [32, 1024, 1024], P('dp', 'ctx')
- first_gain_grad: float32 [1024], P(('dp', 'ctx'))
- first_shift_grad: float32 [1024], P(('dp', 'ctx'))
- second_gain_grad: float32 [1024], P(('dp', 'ctx'))
- second_shift_grad: float32 [1024], P(('dp', 'ctx'))
- project_weight_grad: float32 [1024, 3072], P(('dp', 'ctx'))
- project_bias_grad: float32 [3072], P(('dp', 'ctx'))
- output_weight_grad: float32 [1024, 1024], P(('dp', 'ctx'))
- output_bias_grad: float32 [1024], P(('dp', 'ctx'))
- expand_weight_grad: float32 [1024, 4096], P(('dp', 'ctx'))
- expand_bias_grad: float32 [4096], P(('dp', 'ctx'))
- reduce_weight_grad: float32 [1024, 4, 1024], P(('dp', 'ctx'))
- reduce_bias_grad: float32 [1024], P(('dp', 'ctx'))
The draws below stay inside these ranges and needn't reach their ends.
Inputs may be any that keep to these rules, and one draw needn't show every extreme that they name: Each row is a permutation of the positions of a sequence. The 128 stored rows of ctx index c (rows c * 128 onward) are the positions p * 64 to (p + 1) * 64 - 1 in order, then (15 - p) * 64 to (16 - p) * 64 - 1 in order, where p runs over a permutation of the ctx indices drawn for each sequence.
All inputs are finite; a program needn't handle non-finite values.
Results may differ from the reference program's by a relative error of at most 0.014.
Values may be sent and summed in bfloat16 or wider, within the bound.
A program may use at most 320 MiB of HBM per device.

```python
import jax
import jax.numpy as jnp
from jax import lax

D = 1024
HEADS = 16
HD = 64
ROT = 16
FF = 4096
SEQ_LEN = 1024
GROUPS = 4
STRETCH = 64
SEQS = 32


def draw_positions(key, part):
    key = jax.random.fold_in(key, 7)
    pieces = SEQ_LEN // (2 * STRETCH)
    seq_keys = jax.random.split(key, SEQS)

    def one_row(row_key):
        order = jax.random.permutation(row_key, pieces).astype(jnp.int32)
        earlier = order * STRETCH
        later = (2 * pieces - 1 - order) * STRETCH
        starts = jnp.stack([earlier, later], axis=1)
        inside = jnp.arange(STRETCH, dtype=jnp.int32)
        return (starts[:, :, None] + inside[None, None, :]).reshape(SEQ_LEN)
    return jax.vmap(one_row)(seq_keys).astype(jnp.int32)


def level_of(key, extent, shards, smallest, high):
    def one(dim, blocks):
        heights = jax.random.uniform(jax.random.fold_in(jax.random.fold_in(key, 6), dim), (blocks,), jnp.float32, smallest / len(shards), high / len(shards))
        return jnp.repeat(jnp.exp(heights), extent[dim] // blocks).reshape((-1,) + (1,) * (len(extent) - dim - 1))

    factor_of = one(*shards[0])
    for cut in shards[1:]:
        factor_of = factor_of * one(*cut)
    return factor_of


def scatter_about(own_key, dims, width, reach, cuts=(), kind=jnp.bfloat16):
    values = jax.random.normal(own_key, dims, jnp.float32) * width
    if len(cuts) > 0:
        values = level_of(own_key, dims, cuts, -0.22, 0.18) * values
    return jnp.clip(values, min=-reach, max=reach).astype(kind)


def setup_inputs(seed: int = 0) -> dict:
    key_of = jax.random.split(jax.random.key(seed), 16)
    inputs = scatter_about(key_of[0], (SEQS, SEQ_LEN, D), 1.0, 6.0, ((0, 16), (1, 8)))
    positions = draw_positions(jax.random.fold_in(key_of[15], 71), 0)
    first_gain = jnp.clip(1.0 + 0.1 * jax.random.normal(key_of[2], (D,), jnp.float32), 0.5, 1.5)
    first_shift = scatter_about(key_of[3], (D,), 0.3, 4.0, (), jnp.float32)
    second_gain = jnp.clip(1.0 + 0.1 * jax.random.normal(key_of[4], (D,), jnp.float32), 0.5, 1.5)
    second_shift = scatter_about(key_of[5], (D,), 0.3, 4.0, (), jnp.float32)
    project_weight = scatter_about(key_of[6], (D, 3 * D), D ** -0.5, 0.1875, ((0, 128),))
    project_bias = scatter_about(key_of[7], (3 * D,), 0.5, 4.0, (), jnp.float32)
    output_weight = scatter_about(key_of[8], (D, D), (max(D // 128, 1)) ** -0.5, 2.0, ((0, 128),))
    output_bias = scatter_about(key_of[9], (D,), 0.5, 4.0, (), jnp.float32)
    expand_weight = scatter_about(key_of[10], (D, FF), D ** -0.5, 0.1875, ((0, 128),))
    expand_bias = scatter_about(key_of[11], (FF,), 0.5, 4.0, (), jnp.float32)
    reduce_weight = scatter_about(key_of[12], (D, GROUPS, D), FF ** -0.5, 0.09375, ((0, 128),))
    reduce_bias = scatter_about(key_of[13], (D,), 0.5, 4.0, (), jnp.float32)
    cotangent = scatter_about(key_of[14], (SEQS, SEQ_LEN, D), 1.0, 6.0, ((0, 16), (1, 8)))
    return {"inputs": inputs, "positions": positions, "first_gain": first_gain, "first_shift": first_shift, "second_gain": second_gain, "second_shift": second_shift, "project_weight": project_weight, "project_bias": project_bias, "output_weight": output_weight, "output_bias": output_bias, "expand_weight": expand_weight, "expand_bias": expand_bias, "reduce_weight": reduce_weight, "reduce_bias": reduce_bias, "cotangent": cotangent}


@jax.custom_vjp
def low(v):
    return lax.optimization_barrier(v.astype(jnp.bfloat16)).astype(jnp.float32)

@jax.custom_vjp
def low_back(v):
    return v

def low_keep(v):
    return (low(v), None)

def low_pass(kept, grad):
    return (grad,)

def back_keep(v):
    return (v, None)

def back_low(kept, grad):
    return (low(grad),)
low.defvjp(low_keep, low_pass)
low_back.defvjp(back_keep, back_low)
EPSILON = 1e-05
HIGHEST = lax.Precision.HIGHEST

def normalize(values):
    centred = values - lax.optimization_barrier(jnp.mean(values, axis=-1, keepdims=True))
    return centred * lax.rsqrt(lax.optimization_barrier(jnp.mean(centred * centred, axis=-1, keepdims=True)) + EPSILON)

def rotary_tables(places):
    halfway = ROT // 2
    inverse = 10000.0 ** (-(jnp.arange(halfway, dtype=jnp.float32) * 2.0 / ROT))
    turned = places.astype(jnp.float32)[..., None] * inverse
    return (jnp.cos(turned)[..., None, :], jnp.sin(turned)[..., None, :])

def rotate(tensor, cosine, sine):
    halfway = ROT // 2
    leading = tensor[..., :halfway]
    trailing = tensor[..., halfway:ROT]
    return jnp.concatenate([leading * cosine - trailing * sine, trailing * cosine + leading * sine, tensor[..., ROT:]], axis=-1)

def one_sequence(sequence, places, params):
    first_gain, first_shift, second_gain, second_shift, project_weight, project_bias, output_weight, output_bias, expand_weight, expand_bias, reduce_weight, reduce_bias = params
    length = sequence.shape[0]
    normed = normalize(sequence)
    first_in = low(normed * first_gain + first_shift)
    second_in = low(normed * second_gain + second_shift)
    projected = low_back(jnp.dot(first_in, project_weight, precision=HIGHEST)) + project_bias
    cosine, sine = rotary_tables(places)
    queries = low(rotate(projected[:, :D].reshape(length, HEADS, HD), cosine, sine))
    keys_rot = low(rotate(projected[:, D:2 * D].reshape(length, HEADS, HD), cosine, sine))
    values_seq = low(projected[:, 2 * D:].reshape(length, HEADS, HD))
    scores = low_back(jnp.einsum('qhd,khd->hqk', queries, keys_rot, precision=HIGHEST) * HD ** (-0.5))
    allowed = places[None, :] <= places[:, None]
    scores = jnp.where(allowed[None], scores, -1e+30)
    weights = low(jax.nn.softmax(scores, axis=-1))
    attended = jnp.einsum('hqk,khd->qhd', weights, values_seq, precision=HIGHEST).reshape(length, D)
    attended = low(low_back(attended))
    attention = jnp.dot(attended, output_weight, precision=HIGHEST) + output_bias
    expanded = low_back(jnp.dot(second_in, expand_weight, precision=HIGHEST)) + expand_bias
    activated = low(jax.nn.gelu(expanded, approximate=False))
    reduced = jnp.einsum('lki,ike->le', activated.reshape(length, GROUPS, D), reduce_weight, precision=HIGHEST) + reduce_bias
    return sequence + attention + reduced

def reference(inputs, positions, first_gain, first_shift, second_gain, second_shift, project_weight, project_bias, output_weight, output_bias, expand_weight, expand_bias, reduce_weight, reduce_bias, cotangent):
    params = (first_gain.astype(jnp.float32), first_shift.astype(jnp.float32), second_gain.astype(jnp.float32), second_shift.astype(jnp.float32), project_weight.astype(jnp.float32), project_bias.astype(jnp.float32), output_weight.astype(jnp.float32), output_bias.astype(jnp.float32), expand_weight.astype(jnp.float32), expand_bias.astype(jnp.float32), reduce_weight.astype(jnp.float32), reduce_bias.astype(jnp.float32))

    def forward(every_input, every_param):

        def apply_one(pair):
            return jax.checkpoint(one_sequence)(pair[0], pair[1], every_param)
        return lax.map(apply_one, (every_input, positions))
    output, backward = jax.vjp(forward, inputs.astype(jnp.float32), params)
    input_grad, param_grads = backward(cotangent.astype(jnp.float32))
    return (output.astype(jnp.bfloat16), input_grad.astype(jnp.bfloat16), param_grads[0], param_grads[1], param_grads[2], param_grads[3], param_grads[4], param_grads[5], param_grads[6], param_grads[7], param_grads[8], param_grads[9], param_grads[10], param_grads[11])
```

```python
import functools

import jax
import jax.numpy as jnp
from jax import lax
from jax.experimental import pallas as pl
from jax.experimental.pallas import tpu as pltpu
from jax.sharding import PartitionSpec as P

D = 1024
HEADS = 16
HD = 64
ROT = 16
FF = 4096
GROUPS = 4
EPSILON = 1e-05

RING = 4
TP = 8
SEQ = 4
PART = 128
OWN = 8
QKV = 384
HID = 512
WIDE = QKV + HID

MESH = pl.DeviceIdType.MESH
VMEM = pl.BlockSpec(memory_space=pltpu.VMEM)
BF = jnp.bfloat16
F32 = jnp.float32


def place():
    dp, ctx = lax.axis_index("dp"), lax.axis_index("ctx")
    return ctx % 4, (ctx // 4) * 2 + dp // 8, (dp // 2) % 4, dp % 2


def device(x, y, z, core):
    return {"dp": ((y % 2) * 4 + z) * 2 + core, "ctx": (y // 2) * 4 + x}


class Wire:
    def __init__(self, send, recv):
        self.send, self.recv, self.count = send, recv, 0

    def push(self, src, dst, to):
        i = self.count
        self.count += 1
        copy = pltpu.make_async_remote_copy(
            src_ref=src,
            dst_ref=dst,
            send_sem=self.send.at[i],
            recv_sem=self.recv.at[i],
            device_id=to,
            device_id_type=MESH,
        )
        copy.start()
        return copy


def greet(senders, count):
    barrier = pltpu.get_barrier_semaphore()
    for other in senders:
        pl.semaphore_signal(barrier, inc=1, device_id=other, device_id_type=MESH)
    pl.semaphore_wait(barrier, count)


def row_owner(x, y, z, core):
    ylo = y % 2
    return device(ylo * 2 + z // 2, core * 2 + y // 2, (x + 3 + 2 * ylo) % 4, z % 2)


def row_source(x, y, z, core):
    ylo = x // 2
    return device((z + 1 + 2 * ylo) % 4, (y % 2) * 2 + ylo, (x % 2) * 2 + core, y // 2)


def row_block(x, y, z):
    return y, (z + 1 + 2 * (x // 2)) % 4


def fold(rows):
    return jnp.concatenate([rows[:, : D // 2], rows[:, D // 2 :]], axis=0).astype(BF)


def unfold(rows):
    return jnp.concatenate([rows[:OWN], rows[OWN:]], axis=1)


def gather_kernel(
    x_ref, g_ref, pos_ref, pe_ref, wo_ref, wr_ref,
    xs_out, gs_out, ps_ref, wpe_out, wos_out, wrs_out,
    stage, xs_ref, gs_ref, wpe_ref, wos_ref, wrs_ref, wo_own, wr_own, send, recv, local,
):
    x, y, z, core = place()
    me = (x, y, z, core)
    sib = device(x, y, z, 1 - core)
    xp = [device((x + d) % 4, y, z, core) for d in (1, 2, 3)]
    xq = [device((x + d) % 4, y, z, 1 - core) for d in (1, 2, 3)]
    yp = [device(x, (y + d) % 4, z, core) for d in (1, 2, 3)]
    zp = [device(x, y, (z + d) % 4, core) for d in (1, 2, 3)]
    senders = xp + [sib] + xq + yp + zp + [row_source(*me)]
    mine = pl.ds(2 * core, 2)
    wo_own[...] = fold(wo_ref[...])
    wr_own[...] = wr_ref[...]
    xs_ref[mine, x] = x_ref[...]
    gs_ref[mine, x] = g_ref[...]
    greet(senders, len(senders))
    wire = Wire(send, recv)
    ylo, yhi = y % 2, y // 2
    first = []
    for n, (d, other) in enumerate([(0, sib)] + list(zip((1, 2, 3), xp)) + list(zip((1, 2, 3), xq))):
        same = 1 <= n <= 3
        to_x, to_core = (x + d) % 4, (core if same else 1 - core)
        first.append(
            wire.push(pe_ref.at[to_x * 2 + to_core], stage.at[core, x], other)
        )
    by, bz = row_block(x, y, z)
    owner = row_owner(*me)
    oy, oz = core * 2 + yhi, x
    first_rows = [
        wire.push(wo_own, wos_ref.at[oy, oz], owner),
        wire.push(wr_own, wrs_ref.at[oy, oz], owner),
    ]
    keep = pltpu.make_async_copy(pe_ref.at[x * 2 + core], stage.at[core, x], local.at[0])
    keep.start()
    kp = pltpu.make_async_copy(pos_ref, ps_ref.at[core], local.at[1])
    kp.start()
    ps = wire.push(pos_ref, ps_ref.at[core], sib)
    tok = []
    for d in (1, 3, 2):
        tok.append((d, xs_ref, wire.push(xs_ref.at[mine, x], xs_ref.at[mine, x], xp[d - 1])))
    own = [wire.push(xs_ref.at[mine, x], xs_ref.at[mine, x], sib)]
    for d in (1, 3, 2):
        tok.append((d, gs_ref, wire.push(gs_ref.at[mine, x], gs_ref.at[mine, x], xp[d - 1])))
    own.append(wire.push(gs_ref.at[mine, x], gs_ref.at[mine, x], sib))
    for c in first:
        c.wait()
    keep.wait()
    wpe_ref[ylo, z, :, yhi] = stage[...].reshape(2, 4 * OWN, WIDE).astype(BF)
    for c in first_rows:
        c.wait()
    along_y = []
    for d in (0, 1, 2):
        a = wpe_ref.at[ylo, z, :, yhi]
        b = wos_ref.at[by, bz]
        c = wrs_ref.at[by, bz]
        along_y += [wire.push(a, a, yp[d]), wire.push(b, b, yp[d]), wire.push(c, c, yp[d])]
    for c in along_y:
        c.wait()
    along_z = []
    for d in (0, 1, 2):
        a = wpe_ref.at[:, z]
        b = wos_ref.at[:, bz]
        c = wrs_ref.at[:, bz]
        along_z += [wire.push(a, a, zp[d]), wire.push(b, b, zp[d]), wire.push(c, c, zp[d])]
    on = []
    for d, buf, c in tok:
        c.wait()
        block = buf.at[mine, (x - d + 4) % 4]
        on.append(wire.push(block, block, sib))
    for c in along_z + on + own + [ps]:
        c.wait()
    kp.wait()
    for s, o in ((wpe_ref, wpe_out), (wrs_ref, wrs_out)):
        o[...] = s[...]
    for j in range(16):
        wos_out[j] = unfold(wos_ref[j // 4, j % 4].astype(F32))
    for s, o in ((xs_ref, xs_out), (gs_ref, gs_out)):

        @pl.loop(0, SEQ * RING)
        def _(i):
            o[i // RING, i % RING] = s[i // RING, i % RING]


def gather(inputs, cotangent, positions, pe, wo, wr):
    copies = 7 + 2 + 1 + 8 + 18 + 6
    return pl.pallas_call(
        gather_kernel,
        name="gather",
        out_shape=(
            jax.ShapeDtypeStruct((SEQ, RING, PART, D), BF),
            jax.ShapeDtypeStruct((SEQ, RING, PART, D), BF),
            jax.ShapeDtypeStruct((2, 2, positions.shape[1]), jnp.int32),
            jax.ShapeDtypeStruct((2, 4, 2, 2, 4 * OWN, WIDE), BF),
            jax.ShapeDtypeStruct((16, OWN, D), F32),
            jax.ShapeDtypeStruct((4, 4, GROUPS * OWN, D), BF),
        ),
        in_specs=[VMEM] * 6,
        out_specs=(VMEM,) * 6,
        scratch_shapes=[
            pltpu.VMEM((2, 4, OWN, WIDE), F32),
            pltpu.VMEM((SEQ, RING, PART, D), BF),
            pltpu.VMEM((SEQ, RING, PART, D), BF),
            pltpu.VMEM((2, 4, 2, 2, 4 * OWN, WIDE), BF),
            pltpu.VMEM((4, 4, 2 * OWN, D // 2), BF),
            pltpu.VMEM((4, 4, GROUPS * OWN, D), BF),
            pltpu.VMEM((2 * OWN, D // 2), BF),
            pltpu.VMEM((GROUPS * OWN, D), BF),
            pltpu.SemaphoreType.DMA((copies,)),
            pltpu.SemaphoreType.DMA((copies,)),
            pltpu.SemaphoreType.DMA((2,)),
        ],
        compiler_params=pltpu.CompilerParams(
            collective_id=0, has_side_effects=True, vmem_limit_bytes=56 * 2**20
        ),
    )(inputs, cotangent, positions, pe, wo, wr)


def swap_kernel(src_ref, out_ref, out, into, send, recv):
    x, y, z, core = place()
    other = device(x, (y + 2) % 4, z, core)
    out[...] = src_ref[...]
    greet([other], 1)
    Wire(send, recv).push(out, into, other).wait()
    out_ref[...] = into[...]


def swap(value, number):
    return pl.pallas_call(
        swap_kernel,
        name="swap%d" % number,
        out_shape=jax.ShapeDtypeStruct(value.shape, value.dtype),
        in_specs=[VMEM],
        out_specs=VMEM,
        scratch_shapes=[
            pltpu.VMEM(value.shape, value.dtype),
            pltpu.VMEM(value.shape, value.dtype),
            pltpu.SemaphoreType.DMA((1,)),
            pltpu.SemaphoreType.DMA((1,)),
        ],
        compiler_params=pltpu.CompilerParams(
            collective_id=number, has_side_effects=True, vmem_limit_bytes=56 * 2**20
        ),
    )(value)


def scatter_kernel(
    out_ref, h_ref, pe_arg, wo_arg, wr_arg, small_ref,
    osum_ref, hsum_ref, peg_ref, wog_ref, wrg_ref, smalls_ref,
    away, pe_ref, wo_ref, wr_ref, half, part, ring, pe_in, wo_in, wr_in, pe_b, wo_b, wr_b, pe_in2, wo_in2, wr_in2,
    pe_f, wo_f, wr_f, small_in, small_b, small_g, send, recv, local,
):
    x, y, z, core = place()
    me = (x, y, z, core)
    sib = device(x, y, z, 1 - core)
    xp = [device((x + d) % 4, y, z, core) for d in (1, 2, 3)]
    xq = [device((x + d) % 4, y, z, 1 - core) for d in (1, 2, 3)]
    yp = [device(x, (y + d) % 4, z, core) for d in (1, 2, 3)]
    zp = [device(x, y, (z + d) % 4, core) for d in (1, 2, 3)]
    senders = xp + [sib] + xq + yp + zp + [row_owner(*me)]
    pe_ref[...] = pe_arg[...]
    for j in range(16):
        wo_ref[j // 4, j % 4] = fold(wo_arg[j])
    wr_ref[...] = wr_arg[...]
    for n, r in enumerate((out_ref, h_ref)):

        @pl.loop(0, 2 * RING)
        def _(i):
            s, j = i // RING, i % RING
            away[n, s, j] = r[2 - 2 * core + s, j]

    greet(senders, len(senders))
    wire = Wire(send, recv)
    ylo, yhi = y % 2, y // 2
    by, bz = row_block(x, y, z)
    c0 = [wire.push(away.at[n], half.at[n], sib) for n in range(2)]
    along_z = []
    for d in (0, 1, 2):
        oz = (z + d + 1) % 4
        ob = (bz + d + 1) % 4
        along_z.append(wire.push(pe_ref.at[:, oz], pe_in.at[d], zp[d]))
        along_z.append(wire.push(wo_ref.at[:, ob], wo_in.at[d], zp[d]))
        along_z.append(wire.push(wr_ref.at[:, ob], wr_in.at[d], zp[d]))
    small_z = [wire.push(small_ref, small_in.at[d], zp[d]) for d in (0, 1, 2)]
    sums = []
    for n, (r, o) in enumerate(((out_ref, osum_ref), (h_ref, hsum_ref))):
        c0[n].wait()

        @pl.loop(0, 2 * RING)
        def _(i):
            s, j = i // RING, i % RING
            part[n, s, j] = (
                r[2 * core + s, j].astype(F32) + half[n, s, j].astype(F32)
            ).astype(BF)

        for d in (0, 1, 2):
            sums.append(
                wire.push(part.at[n, :, (x + d + 1) % 4], ring.at[n, d], xp[d])
            )
    for c in along_z + small_z:
        c.wait()
    pe_b[...] = (
        pe_ref[:, z].astype(F32) + pe_in[0].astype(F32) + pe_in[1].astype(F32) + pe_in[2].astype(F32)
    ).astype(BF)
    wo_b[...] = (
        wo_ref[:, bz].astype(F32) + wo_in[0].astype(F32) + wo_in[1].astype(F32) + wo_in[2].astype(F32)
    ).astype(BF)
    wr_b[...] = (
        wr_ref[:, bz].astype(F32) + wr_in[0].astype(F32) + wr_in[1].astype(F32) + wr_in[2].astype(F32)
    ).astype(BF)
    small_b[...] = small_ref[...] + small_in[0] + small_in[1] + small_in[2]
    along_y = []
    for d in (0, 1, 2):
        oy = (y + d + 1) % 4
        along_y.append(wire.push(pe_b.at[oy % 2, :, oy // 2], pe_in2.at[d], yp[d]))
        along_y.append(wire.push(wo_b.at[oy], wo_in2.at[d], yp[d]))
        along_y.append(wire.push(wr_b.at[oy], wr_in2.at[d], yp[d]))
        along_y.append(wire.push(small_b, small_in.at[3 + d], yp[d]))
    for c in along_y:
        c.wait()
    pe_f[...] = (
        pe_b[ylo, :, yhi].astype(F32)
        + pe_in2[0].astype(F32)
        + pe_in2[1].astype(F32)
        + pe_in2[2].astype(F32)
    ).reshape(2, 4, OWN, WIDE)
    wo_f[...] = unfold(
        wo_b[y].astype(F32)
        + wo_in2[0].astype(F32)
        + wo_in2[1].astype(F32)
        + wo_in2[2].astype(F32)
    )
    wr_f[...] = wr_b[y].astype(F32) + wr_in2[0].astype(F32) + wr_in2[1].astype(F32) + wr_in2[2].astype(F32)
    small_g[...] = small_b[...] + small_in[3] + small_in[4] + small_in[5]
    t = x * 2 + core
    last = []
    for n, (d, other) in enumerate([(0, sib)] + list(zip((1, 2, 3), xp)) + list(zip((1, 2, 3), xq))):
        same = 1 <= n <= 3
        to_x, to_core = (x + d) % 4, (core if same else 1 - core)
        last.append(wire.push(pe_f.at[to_core, to_x], peg_ref.at[t], other))
        last.append(wire.push(small_g, smalls_ref.at[t], other))
    source = row_source(*me)
    last.append(wire.push(wo_f, wog_ref, source))
    last.append(wire.push(wr_f, wrg_ref, source))
    k0 = pltpu.make_async_copy(pe_f.at[core, x], peg_ref.at[t], local.at[0])
    k1 = pltpu.make_async_copy(small_g, smalls_ref.at[t], local.at[1])
    k0.start()
    k1.start()
    for n, (r, o) in enumerate(((out_ref, osum_ref), (h_ref, hsum_ref))):
        for c in sums[3 * n : 3 * n + 3]:
            c.wait()
        for s in range(2):
            o[s] = (
                part[n, s, x].astype(F32)
                + ring[n, 0, s].astype(F32)
                + ring[n, 1, s].astype(F32)
                + ring[n, 2, s].astype(F32)
            )
    for c in last:
        c.wait()
    k0.wait()
    k1.wait()


def scatter(out, h, pe, wo, wr, small):
    copies = 2 + 9 + 3 + 6 + 12 + 14 + 2
    sr = small.shape
    return pl.pallas_call(
        scatter_kernel,
        name="scatter",
        out_shape=(
            jax.ShapeDtypeStruct((2, PART, D), F32),
            jax.ShapeDtypeStruct((2, PART, D), F32),
            jax.ShapeDtypeStruct((TP, OWN, WIDE), F32),
            jax.ShapeDtypeStruct((OWN, D), F32),
            jax.ShapeDtypeStruct((GROUPS * OWN, D), F32),
            jax.ShapeDtypeStruct((TP,) + sr, F32),
        ),
        in_specs=[VMEM] * 6,
        out_specs=(VMEM,) * 6,
        scratch_shapes=[
            pltpu.VMEM((2, 2, RING, PART, D), BF),
            pltpu.VMEM((2, 4, 2, 2, 4 * OWN, WIDE), BF),
            pltpu.VMEM((4, 4, 2 * OWN, D // 2), BF),
            pltpu.VMEM((4, 4, GROUPS * OWN, D), BF),
            pltpu.VMEM((2, 2, RING, PART, D), BF),
            pltpu.VMEM((2, 2, RING, PART, D), BF),
            pltpu.VMEM((2, 3, 2, PART, D), BF),
            pltpu.VMEM((3, 2, 2, 2, 4 * OWN, WIDE), BF),
            pltpu.VMEM((3, 4, 2 * OWN, D // 2), BF),
            pltpu.VMEM((3, 4, GROUPS * OWN, D), BF),
            pltpu.VMEM((2, 2, 2, 4 * OWN, WIDE), BF),
            pltpu.VMEM((4, 2 * OWN, D // 2), BF),
            pltpu.VMEM((4, GROUPS * OWN, D), BF),
            pltpu.VMEM((3, 2, 4 * OWN, WIDE), BF),
            pltpu.VMEM((3, 2 * OWN, D // 2), BF),
            pltpu.VMEM((3, GROUPS * OWN, D), BF),
            pltpu.VMEM((2, 4, OWN, WIDE), F32),
            pltpu.VMEM((OWN, D), F32),
            pltpu.VMEM((GROUPS * OWN, D), F32),
            pltpu.VMEM((6,) + sr, F32),
            pltpu.VMEM(sr, F32),
            pltpu.VMEM(sr, F32),
            pltpu.SemaphoreType.DMA((copies,)),
            pltpu.SemaphoreType.DMA((copies,)),
            pltpu.SemaphoreType.DMA((2,)),
        ],
        compiler_params=pltpu.CompilerParams(
            collective_id=3, has_side_effects=True, vmem_limit_bytes=60 * 2**20
        ),
    )(out, h, pe, wo, wr, small)


def rotary_tables(places):
    halfway = ROT // 2
    inverse = 10000.0 ** (-(jnp.arange(halfway, dtype=F32) * 2.0 / ROT))
    turned = places.astype(F32)[..., None] * inverse
    return (jnp.cos(turned)[..., None, :], jnp.sin(turned)[..., None, :])


def rotate(tensor, cosine, sine):
    halfway = ROT // 2
    leading = tensor[..., :halfway]
    trailing = tensor[..., halfway:ROT]
    return jnp.concatenate(
        [leading * cosine - trailing * sine, trailing * cosine + leading * sine, tensor[..., ROT:]],
        axis=-1,
    )


def across(left, right):
    return lax.dot_general(left, right, (((1,), (1,)), ((), ())), preferred_element_type=F32)


def down_rows(left, right):
    return lax.dot_general(left, right, (((0,), (0,)), ((), ())), preferred_element_type=F32)


def shards(
    inputs, positions, first_gain, first_shift, second_gain, second_shift, project_weight,
    project_bias, output_weight, output_bias, expand_weight, expand_bias, reduce_weight,
    reduce_bias, cotangent,
):
    x, y, z, core = place()
    t = x * 2 + core
    yhi = y // 2
    full = positions.shape[1]
    half = full // 2
    scaling = HD ** (-0.5)
    rows = SEQ * RING * PART
    pe = jnp.concatenate(
        [
            project_weight.reshape(OWN, 3, TP, 128),
            expand_weight.reshape(OWN, GROUPS, TP, 128),
        ],
        axis=1,
    ).transpose(2, 0, 1, 3).reshape(TP, OWN, WIDE).astype(F32)
    wr32 = reduce_weight.transpose(1, 0, 2).reshape(GROUPS * OWN, D)
    xs, gs, ps, wpe, wos, wrs = gather(inputs, cotangent, positions, pe, output_weight.astype(F32), wr32)
    widened = xs.astype(F32).reshape(rows, D)
    upstream = gs.reshape(rows, D)
    wpe = wpe.reshape(D, WIDE)
    wp, we = wpe[:, :QKV], wpe[:, QKV:]
    wo = wos.reshape(128, D).astype(BF)
    wr = wrs.reshape(16, GROUPS, OWN, D).transpose(1, 0, 2, 3).reshape(HID, D)
    bp = lax.dynamic_slice_in_dim(project_bias.reshape(3, TP, 128), t, 1, 1).reshape(QKV)
    be = lax.dynamic_slice_in_dim(expand_bias.reshape(GROUPS, TP, 128), t, 1, 1).reshape(HID)
    places = ps.reshape(SEQ, full)
    local_places = lax.dynamic_slice_in_dim(places, yhi * half, half, 1)

    centred = widened - jnp.mean(widened, axis=-1, keepdims=True)
    inv_scale = lax.rsqrt(jnp.mean(centred * centred, axis=-1, keepdims=True) + EPSILON)
    normed = centred * inv_scale
    first_in = (normed * first_gain + first_shift).astype(BF)
    second_in = (normed * second_gain + second_shift).astype(BF)
    projected = jnp.dot(first_in, wp, preferred_element_type=F32) + bp
    cosine, sine = rotary_tables(local_places)
    queries = rotate(projected[:, :128].reshape(SEQ, half, 2, HD), cosine, sine).astype(BF)
    keys = rotate(projected[:, 128:256].reshape(SEQ, half, 2, HD), cosine, sine).astype(BF)
    values = projected[:, 256:].reshape(SEQ, half, 128).astype(BF)
    kv = jnp.concatenate([keys.reshape(SEQ, half, 128), values], axis=-1)
    kv_other = swap(kv, 1)
    kv_all = jnp.concatenate([kv, kv_other], axis=1)
    key_heads = kv_all[..., :128].reshape(SEQ, full, 2, HD)
    value_heads = kv_all[..., 128:].reshape(SEQ, full, 2, HD)
    key_places = jnp.concatenate(
        [local_places, lax.dynamic_slice_in_dim(places, (1 - yhi) * half, half, 1)], axis=1
    )
    allowed = key_places[:, None, None, :] <= local_places[:, None, :, None]
    scores = (
        jnp.einsum("mqhd,mkhd->mhqk", queries, key_heads, preferred_element_type=F32) * scaling
    )
    scores = jnp.where(allowed, scores, -1e30)
    highest = jnp.max(scores, axis=-1, keepdims=True)
    raised = jnp.exp(scores - highest)
    denominator = jnp.sum(raised, axis=-1, keepdims=True)
    probs = raised / denominator
    probs_low = probs.astype(BF)
    attended_low = (
        jnp.einsum("mhqk,mkhd->mqhd", probs_low, value_heads, preferred_element_type=F32)
        .reshape(rows, 128)
        .astype(BF)
    )
    expanded = jnp.dot(second_in, we, preferred_element_type=F32) + be
    hidden, gelu_back = jax.vjp(lambda v: jax.nn.gelu(v, approximate=False), expanded)
    hidden_low = hidden.astype(BF)
    out_part = jnp.dot(attended_low, wo, preferred_element_type=F32) + jnp.dot(
        hidden_low, wr, preferred_element_type=F32
    )
    d_attended = across(upstream, wo)
    d_hidden = across(upstream, wr)
    d_expanded = gelu_back(d_hidden)[0]
    d_expanded_low = d_expanded.astype(BF)
    d_out = d_attended.astype(BF).reshape(SEQ, half, 2, HD)
    d_probs = jnp.einsum("mqhd,mkhd->mhqk", d_out, value_heads, preferred_element_type=F32)
    row_delta = jnp.sum(d_probs * probs, axis=-1, keepdims=True)
    d_scores = (probs * (d_probs - row_delta)).astype(BF)
    d_queries = (
        jnp.einsum("mhqk,mkhd->mqhd", d_scores, key_heads, preferred_element_type=F32) * scaling
    )
    d_keys = (
        jnp.einsum("mhqk,mqhd->mkhd", d_scores, queries, preferred_element_type=F32) * scaling
    ).reshape(SEQ, full, 128)
    d_values = jnp.einsum("mhqk,mqhd->mkhd", probs_low, d_out, preferred_element_type=F32).reshape(
        SEQ, full, 128
    )
    d_kv = jnp.concatenate([d_keys, d_values], axis=-1)
    d_kv = d_kv[:, :half] + swap(d_kv[:, half:].astype(BF), 2).astype(F32)
    query_back = rotate(d_queries, cosine, -sine).reshape(rows, 128)
    key_back = rotate(d_kv[..., :128].reshape(SEQ, half, 2, HD), cosine, -sine).reshape(rows, 128)
    d_projected = jnp.concatenate([query_back, key_back, d_kv[..., 128:].reshape(rows, 128)], axis=1)
    d_projected_low = d_projected.astype(BF)
    d_first = across(d_projected_low, wp)
    d_second = across(d_expanded_low, we)
    h_part = d_first * first_gain + d_second * second_gain
    g_own = cotangent.astype(F32)
    tail = jnp.concatenate([jnp.sum(d_projected, axis=0), jnp.sum(d_expanded, axis=0), jnp.zeros(D - WIDE, F32)])
    zero = jnp.zeros(D, F32)
    small = jnp.stack(
        [
            jnp.sum(d_first * normed, axis=0),
            jnp.sum(d_first, axis=0),
            jnp.sum(d_second * normed, axis=0),
            jnp.sum(d_second, axis=0),
            jnp.sum(g_own, axis=(0, 1)),
            tail,
            zero,
            zero,
        ]
    )
    pe_grad = jnp.concatenate(
        [down_rows(first_in, d_projected_low), down_rows(second_in, d_expanded_low)], axis=1
    ).astype(BF)
    wo_grad = down_rows(attended_low, upstream).reshape(16, OWN, D)
    wr_grad = down_rows(hidden_low, upstream).astype(BF)
    wr_grad = (
        wr_grad.reshape(GROUPS, 16, OWN, D).transpose(1, 0, 2, 3).reshape(4, 4, GROUPS * OWN, D)
    )
    osum, hsum, peg, wog, wrg, smalls = scatter(
        out_part.astype(BF).reshape(SEQ, RING, PART, D),
        h_part.astype(BF).reshape(SEQ, RING, PART, D),
        pe_grad.reshape(2, 4, 2, 2, 4 * OWN, WIDE),
        wo_grad,
        wr_grad,
        small,
    )
    own = inputs.astype(F32)
    block_output = (own + osum + output_bias + reduce_bias).astype(BF)
    centred = own - jnp.mean(own, axis=-1, keepdims=True)
    inv_scale = lax.rsqrt(jnp.mean(centred * centred, axis=-1, keepdims=True) + EPSILON)
    normed = centred * inv_scale
    inputs_grad = (
        g_own
        + inv_scale
        * (
            hsum
            - jnp.mean(hsum, axis=-1, keepdims=True)
            - normed * jnp.mean(hsum * normed, axis=-1, keepdims=True)
        )
    ).astype(BF)
    peg = peg.reshape(TP, OWN, 7, 128).transpose(1, 2, 0, 3)
    project_weight_grad = peg[:, :3].reshape(OWN, 3 * D)
    expand_weight_grad = peg[:, 3:].reshape(OWN, FF)
    output_weight_grad = wog
    reduce_weight_grad = wrg.reshape(GROUPS, OWN, D).transpose(1, 0, 2)
    index = lax.axis_index("dp") * 8 + lax.axis_index("ctx")
    whole = jnp.sum(smalls[:, :5], axis=0)
    vec = lax.dynamic_slice_in_dim(whole, index * 8, 8, 1)
    table = smalls[:, 5, :WIDE].reshape(TP, 7, 128).transpose(1, 0, 2)
    project_bias_grad = lax.dynamic_slice_in_dim(table[:3].reshape(3 * D), index * 24, 24, 0)
    expand_bias_grad = lax.dynamic_slice_in_dim(table[3:].reshape(FF), index * 32, 32, 0)
    return (
        block_output,
        inputs_grad,
        vec[0],
        vec[1],
        vec[2],
        vec[3],
        project_weight_grad,
        project_bias_grad,
        output_weight_grad,
        vec[4],
        expand_weight_grad,
        expand_bias_grad,
        reduce_weight_grad,
        vec[4],
    )


def solution(mesh):
    rows = P(("dp", "ctx"), None)
    vector = P(("dp", "ctx"))
    tokens = P("dp", "ctx", None)
    deep = P(("dp", "ctx"), None, None)
    return jax.shard_map(
        shards,
        mesh=mesh,
        in_specs=(
            tokens, P("dp", None), P(), P(), P(), P(), rows, P(), rows, P(), rows, P(), deep, P(),
            tokens,
        ),
        out_specs=(
            tokens, tokens, vector, vector, vector, vector, rows, vector, rows, vector, rows,
            vector, deep, vector,
        ),
        check_vma=False,
    )
```

```python
import jax
import jax.numpy as jnp
import numpy as np
from jax import lax
from jax.experimental import pallas as pl
from jax.experimental.pallas import tpu as pltpu
from jax.sharding import PartitionSpec as P

D = 1024
HD = 64
ROT = 16
FF = 4096
GROUPS = 4
EPSILON = 1e-05

RING = 4
TP = 8
SEQ = 4
PART = 128
HALF = RING * PART
FULL = 2 * HALF
OWN = 8
LANES = 128
QKV = 3 * LANES
HID = GROUPS * LANES
WIDE = QKV + HID
SCALE = HD ** (-0.5)
BLOCK = 256

MESH = pl.DeviceIdType.MESH
VMEM = pl.BlockSpec(memory_space=pltpu.VMEM)
BF = jnp.bfloat16
F32 = jnp.float32


def place():
    dp, ctx = lax.axis_index("dp"), lax.axis_index("ctx")
    return ctx % 4, (ctx // 4) * 2 + dp // 8, (dp // 2) % 4, dp % 2


def device(x, y, z, core):
    return {"dp": ((y % 2) * 4 + z) * 2 + core, "ctx": (y // 2) * 4 + x}


class Wire:
    def __init__(self, send, recv):
        self.send, self.recv, self.copies = send, recv, []

    def push(self, src, dst, to):
        i = len(self.copies)
        copy = pltpu.make_async_remote_copy(
            src_ref=src,
            dst_ref=dst,
            send_sem=self.send.at[i],
            recv_sem=self.recv.at[i],
            device_id=to,
            device_id_type=MESH,
        )
        copy.start()
        self.copies.append(copy)
        return copy


def greet(senders, count):
    barrier = pltpu.get_barrier_semaphore()
    for other in senders:
        pl.semaphore_signal(barrier, inc=1, device_id=other, device_id_type=MESH)
    pl.semaphore_wait(barrier, count)


def row_owner(x, y, z, core):
    ylo = y % 2
    return device(ylo * 2 + z // 2, core * 2 + y // 2, (x + 3 + 2 * ylo) % 4, z % 2)


def row_source(x, y, z, core):
    ylo = x // 2
    return device((z + 1 + 2 * ylo) % 4, (y % 2) * 2 + ylo, (x % 2) * 2 + core, y // 2)


def row_block(x, y, z):
    return y, (z + 1 + 2 * (x // 2)) % 4


def fold(rows):
    return jnp.concatenate([rows[:, : D // 2], rows[:, D // 2 :]], axis=0).astype(BF)


def unfold(rows):
    return jnp.concatenate([rows[:OWN], rows[OWN:]], axis=1)


def mul(a, b, ca=1, cb=0):
    return lax.dot_general(a, b, (((ca,), (cb,)), ((), ())), preferred_element_type=F32)


def lane_of(rows):
    return lax.broadcasted_iota(jnp.int32, (rows, LANES), 1)


def turn(v, cosine, sine):
    low = lane_of(v.shape[0]) % HD < ROT // 2
    mate = jnp.where(low, pltpu.roll(v, LANES - ROT // 2, 1), pltpu.roll(v, ROT // 2, 1))
    return v * cosine + mate * sine


def column(row):
    r = lax.broadcasted_iota(jnp.int32, (PART, PART), 0)
    c = lax.broadcasted_iota(jnp.int32, (PART, PART), 1)
    return jnp.sum(jnp.where(r == c, row, 0.0), axis=1, keepdims=True)


def colsum(v):
    return jnp.sum(v, axis=0, keepdims=True)


SCRATCH = dict(
    pe_s=((TP, OWN, WIDE), F32),
    stage=((2, 4, OWN, WIDE), F32),
    wpe=((2, 4, 2, 2, 4 * OWN, WIDE), BF),
    wo_own=((2 * OWN, D // 2), BF),
    wr_f=((GROUPS, OWN, D), F32),
    wr_own=((GROUPS * OWN, D), BF),
    wos=((4, 4, 2 * OWN, D // 2), BF),
    wrs=((4, 4, GROUPS * OWN, D), BF),
    wo=((LANES, D), BF),
    wr=((HID, D), BF),
    xs=((SEQ, RING, PART, D), BF),
    gs=((SEQ, RING, PART, D), BF),
    ps=((2, 8, FULL), F32),
    first=((SEQ, RING, PART, D), BF),
    second=((SEQ, RING, PART, D), BF),
    tab=((SEQ, RING, PART, LANES), F32),
    qs=((SEQ, RING, PART, LANES), BF),
    kv=((2, SEQ, 2, RING, PART, LANES), BF),
    att=((SEQ, HALF, LANES), BF),
    hid=((SEQ, RING, PART, HID), BF),
    dexp=((SEQ, RING, PART, HID), BF),
    datt=((SEQ, RING, PART, LANES), BF),
    dkv_own=((SEQ, 2, LANES, HALF), F32),
    dkv_out=((SEQ, 2, LANES, HALF), BF),
    dkv_in=((SEQ, 2, LANES, HALF), BF),
    dproj=((SEQ, HALF, QKV), BF),
    ob=((2, 2, RING, PART, D), BF),
    half=((2, RING, PART, D), BF),
    ring_o=((2, 3, PART, D), BF),
    ring_h=((2, 3, PART, D), BF),
    small=((8, D), F32),
    small_in=((6, 8, D), F32),
    small_b=((8, D), F32),
    small_g=((8, D), F32),
    small_all=((TP, 8, D), F32),
    rg_z=((3, 4, GROUPS * OWN, D), BF),
    rg_b=((4, GROUPS * OWN, D), BF),
    rg_y=((3, GROUPS * OWN, D), BF),
    rg_f=((GROUPS * OWN, D), F32),
    rg_all=((GROUPS * OWN, D), F32),
    og_z=((3, 4, 2 * OWN, D // 2), BF),
    og_b=((4, 2 * OWN, D // 2), BF),
    og_y=((3, 2 * OWN, D // 2), BF),
    og_f=((OWN, D), F32),
    eg=((2, 4, 2, 2, 4 * OWN, HID), BF),
    eg_z=((3, 2, 2, 2, 4 * OWN, HID), BF),
    eg_b=((2, 2, 2, 4 * OWN, HID), BF),
    eg_y=((3, 2, 4 * OWN, HID), BF),
    eg_f=((2, 4, OWN, HID), F32),
    eg_all=((TP, OWN, HID), F32),
    pg=((2, 4, 2, 2, 4 * OWN, QKV), BF),
    pg_z=((3, 2, 2, 2, 4 * OWN, QKV), BF),
    pg_b=((2, 2, 2, 4 * OWN, QKV), BF),
    pg_y=((3, 2, 4 * OWN, QKV), BF),
    pg_f=((2, 4, OWN, QKV), F32),
    pg_all=((TP, OWN, QKV), F32),
)
COPIES = 176


def block_kernel(
    x_ref, g_ref, pos_ref, inv_ref, g1, s1, g2, s2, pw_ref, bp_ref, ow_ref, bo_ref, ew_ref, be_ref,
    rw_ref, br_ref,
    out_ref, dx_ref, pwg_ref, owg_ref, ewg_ref, rwg_ref, whole_ref, table_ref,
    *scratch,
):
    b = dict(zip(SCRATCH, scratch))
    send, recv = scratch[len(SCRATCH) :]
    xs, gs, ps, first, second, tab = (b[n] for n in ("xs", "gs", "ps", "first", "second", "tab"))
    wpe, wos, wrs, wo, wr, kv = (b[n] for n in ("wpe", "wos", "wrs", "wo", "wr", "kv"))
    small = b["small"]
    x, y, z, core = place()
    me = (x, y, z, core)
    t = x * 2 + core
    ylo, yhi = y % 2, y // 2
    sib = device(x, y, z, 1 - core)
    xp = [device((x + d) % 4, y, z, core) for d in (1, 2, 3)]
    xq = [device((x + d) % 4, y, z, 1 - core) for d in (1, 2, 3)]
    yp = [device(x, (y + d) % 4, z, core) for d in (1, 2, 3)]
    zp = [device(x, y, (z + d) % 4, core) for d in (1, 2, 3)]
    mine = pl.ds(2 * core, 2)
    group = [(x, 1 - core, sib)]
    group += [((x + d) % 4, core, xp[d - 1]) for d in (1, 2, 3)]
    group += [((x + d) % 4, 1 - core, xq[d - 1]) for d in (1, 2, 3)]
    t128 = pl.multiple_of(t * LANES, LANES)

    pw, ew = pw_ref[...].astype(F32), ew_ref[...].astype(F32)
    for u in range(TP):
        for m in range(3):
            b["pe_s"][u, :, m * LANES : (m + 1) * LANES] = pw[:, m * D + u * LANES : m * D + (u + 1) * LANES]
        for k in range(GROUPS):
            at = QKV + k * LANES
            b["pe_s"][u, :, at : at + LANES] = ew[:, k * D + u * LANES : k * D + (u + 1) * LANES]
    b["wo_own"][...] = fold(ow_ref[...].astype(F32))
    for i in range(OWN):
        b["wr_f"][:, i, :] = rw_ref[i].astype(F32)
    b["wr_own"][...] = b["wr_f"][...].reshape(GROUPS * OWN, D).astype(BF)
    xs[mine, x] = x_ref[...]
    gs[mine, x] = g_ref[...]
    ps[...] = jnp.zeros_like(ps)
    ps[core, 0:2] = pos_ref[...].astype(F32)
    small[...] = jnp.zeros_like(small)
    tab[...] = jnp.zeros_like(tab)

    senders = xp + [sib] + xq + yp + zp + [row_source(*me), row_owner(*me)]
    greet(senders, len(senders))
    wire = Wire(send, recv)
    push = wire.push

    step = [push(b["pe_s"].at[ux * 2 + uc], b["stage"].at[core, x], other) for ux, uc, other in group]
    by, bz = row_block(*me[:3])
    owner = row_owner(*me)
    oy, oz = core * 2 + yhi, x
    step_rows = [
        push(b["wo_own"], wos.at[oy, oz], owner),
        push(b["wr_own"], wrs.at[oy, oz], owner),
    ]
    sp = push(ps.at[core], ps.at[core], sib)
    own = xs.at[mine, x]
    xc = [push(own, own, xp[0]), push(own, own, xp[2]), push(own, own, sib)]
    b["stage"][core, x] = b["pe_s"][t]

    def keep_turn(s, j, v, turning):
        tab[s, j] = jnp.where((lane_of(PART) % HD < ROT) == turning, v, tab[s, j])

    def angles(v):
        lane, back = lane_of(v.shape[0]), pltpu.roll(v, HD, 1)
        turned = lane % HD < ROT
        cosine = jnp.where(turned, jnp.where(lane < HD, v, back), 1.0)
        return cosine, jnp.where(turned, jnp.where(lane < HD, back, v), 0.0)

    def layer_norm(s0, count, j):
        @pl.loop(0, count)
        def _(i):
            s = s0 + i
            v = xs[s, j].astype(F32)
            mean = jnp.mean(v, axis=1, keepdims=True)
            c = v - mean
            r = lax.rsqrt(jnp.mean(c * c, axis=1, keepdims=True) + EPSILON)
            n = c * r
            first[s, j] = (n * g1[...] + s1[...]).astype(BF)
            second[s, j] = (n * g2[...] + s2[...]).astype(BF)
            keep_turn(s, j, jnp.where(lane_of(PART) < HD, mean, r), False)

    def tables(s):
        @pl.loop(0, RING)
        def _(j):
            row = ps[s // 2, s % 2 : s % 2 + 1, pl.ds(pl.multiple_of(yhi * HALF + j * PART, PART), PART)]
            angle = column(row) * inv_ref[...]
            lane = lane_of(PART)
            sign = jnp.where(lane % HD < ROT // 2, -1.0, 1.0)
            keep_turn(s, j, jnp.where(lane < HD, jnp.cos(angle), jnp.sin(angle) * sign), True)

    bias_p = jnp.concatenate([bp_ref[:, pl.ds(pl.multiple_of(m * D + t128, LANES), LANES)] for m in range(3)], axis=1)
    bias_e = jnp.concatenate(
        [be_ref[:, pl.ds(pl.multiple_of(k * D + t128, LANES), LANES)] for k in range(GROUPS)], axis=1
    )

    def project(j):
        p = mul(first[:, j].reshape(HALF, D), wpe[:, :, :, :, :, 0:QKV].reshape(D, QKV)) + bias_p
        c, s = angles(tab[:, j].reshape(HALF, LANES))
        shape = (SEQ, PART, LANES)
        b["qs"][:, j] = turn(p[:, :LANES], c, s).astype(BF).reshape(shape)
        kv[0, :, 0, j] = turn(p[:, LANES : 2 * LANES], c, s).astype(BF).reshape(shape)
        kv[1, :, 0, j] = p[:, 2 * LANES :].astype(BF).reshape(shape)
        return push(kv.at[:, :, 0, j], kv.at[:, :, 1, j], yp[1])

    def expand(j):
        e = mul(second[:, j].reshape(HALF, D), wpe[:, :, :, :, :, QKV:].reshape(D, HID)) + bias_e
        cdf = 0.5 * (1.0 + lax.erf(e * 0.5**0.5))
        b["hid"][:, j] = (e * cdf).astype(BF).reshape(SEQ, PART, HID)
        slope = cdf + e * (jnp.exp(-0.5 * e * e) * (2.0 * np.pi) ** -0.5)
        b["dexp"][:, j] = slope.astype(BF).reshape(SEQ, PART, HID)

    layer_norm(2 * core, 2, x)
    for c in step:
        c.wait_recv()
    wpe[ylo, z, :, yhi] = b["stage"][...].reshape(2, 4 * OWN, WIDE).astype(BF)
    for c in step_rows:
        c.wait_recv()
    top, low = pl.ds(0, 2 * OWN), pl.ds(2 * OWN, 2 * OWN)
    stage1 = []
    for d in (0, 2, 1):
        v = wpe.at[ylo, z, 0, yhi]
        stage1.append(push(v, v, yp[d]))
        v = wpe.at[ylo, z, 1, yhi]
        stage1.append(push(v, v, zp[d]))
    rows1 = []
    for d in (0, 2, 1):
        v = wrs.at[by, bz, top]
        rows1.append(push(v, v, yp[d]))
        v = wrs.at[by, bz, low]
        rows1.append(push(v, v, zp[d]))
        v = wos.at[by, bz]
        rows1.append(push(v, v, yp[d]))
    sp.wait_recv()
    for s in range(SEQ):
        tables(s)
    xc[2].wait_recv()
    layer_norm(2 - 2 * core, 2, x)
    for c in stage1:
        c.wait_recv()
    stage2 = []
    for d in (0, 2, 1):
        v = wpe.at[:, z, 0]
        stage2.append(push(v, v, zp[d]))
        v = wpe.at[ylo, :, 1, yhi]
        stage2.append(push(v, v, yp[d]))
    for c in rows1:
        c.wait_recv()
    rows2 = []
    for d in (0, 2, 1):
        v = wrs.at[:, bz, top]
        rows2.append(push(v, v, zp[d]))
        v = wrs.at[by, :, low]
        rows2.append(push(v, v, yp[d]))
        v = wos.at[:, bz]
        rows2.append(push(v, v, zp[d]))
    before, after, far = (x + 3) % 4, (x + 1) % 4, (x + 2) % 4

    def relay(buf, near):
        near[0].wait_recv()
        v = buf.at[2 * core, before]
        ahead = push(v, v, xp[0])
        near[1].wait_recv()
        v = buf.at[2 * core + 1, after]
        back = push(v, v, xp[2])
        v, w = buf.at[mine, before], buf.at[mine, after]
        return [ahead, back], [push(v, v, sib), push(w, w, sib)]

    def relay_far(buf, fars):
        fars[0].wait_recv()
        v = buf.at[2 * core, far]
        a = push(v, v, sib)
        fars[1].wait_recv()
        w = buf.at[2 * core + 1, far]
        return [a, push(w, w, sib)]

    xf, xd = relay(xs, xc)
    own = gs.at[mine, x]
    gc = [push(own, own, xp[0]), push(own, own, xp[2]), push(own, own, sib)]
    layer_norm(2 * core, 2, before)
    layer_norm(2 * core, 2, after)
    for c in xd:
        c.wait_recv()
    layer_norm(2 - 2 * core, 2, before)
    layer_norm(2 - 2 * core, 2, after)
    for c in stage2:
        c.wait_recv()
    kc = [project(x), project(before), project(after)]
    xfd = relay_far(xs, xf)
    expand(x)
    layer_norm(2 * core, 2, far)
    for c in xfd:
        c.wait_recv()
    layer_norm(2 - 2 * core, 2, far)
    kc.append(project(far))
    expand(before)
    gf, gd = relay(gs, gc)
    expand(after)
    expand(far)

    for c in rows2:
        c.wait_recv()
    for j in range(16):
        wo_f = unfold(wos[j // 4, j % 4].astype(F32))
        b["wr_f"][0] = wo_f
        if j % 2 == 0:
            last = wo_f
        else:
            wo[(j - 1) * OWN : (j + 1) * OWN] = jnp.concatenate([last, wo_f], axis=0).astype(BF)
    wr_all = wrs[...].reshape(16, GROUPS, OWN, D).astype(F32)
    for k in range(GROUPS):
        wr[k * LANES : (k + 1) * LANES] = wr_all[:, k].reshape(LANES, D).astype(BF)

    small[4:5] = colsum(g_ref[...].astype(F32).reshape(2 * PART, D))

    def upstream(j):
        g = gs[:, j].reshape(HALF, D)
        b["datt"][:, j] = mul(g, wo[...], 1, 1).astype(BF).reshape(SEQ, PART, LANES)
        d = mul(g, wr[...], 1, 1) * b["dexp"][:, j].reshape(HALF, HID).astype(F32)
        small[5:6, QKV:WIDE] += colsum(d)
        b["dexp"][:, j] = d.astype(BF).reshape(SEQ, PART, HID)

    gc[2].wait_recv()
    for c in gd:
        c.wait_recv()
    gfd = relay_far(gs, gf)
    upstream(x)
    upstream(before)
    upstream(after)
    for c in gfd:
        c.wait_recv()
    upstream(far)
    settled = xc + xf + xd + xfd + step_rows + rows1 + rows2
    for c in settled:
        c.wait_send()
    for c in kc:
        c.wait_recv()

    def attend(s):
        k, v = kv[0, s].reshape(FULL, LANES), kv[1, s].reshape(FULL, LANES)
        row = ps[s // 2, pl.ds(s % 2, 1), pl.ds(pl.multiple_of(yhi * HALF, HALF), HALF)]
        other = ps[s // 2, pl.ds(s % 2, 1), pl.ds(pl.multiple_of((1 - yhi) * HALF, HALF), HALF)]
        keys_at = jnp.concatenate([row, other], axis=1)
        lane = lane_of(BLOCK)
        zero = jnp.zeros((BLOCK, LANES), BF)
        dk = dv = None
        for i in range(HALF // BLOCK):
            few = slice(i * BLOCK // PART, (i + 1) * BLOCK // PART)
            at_rows = slice(i * BLOCK, (i + 1) * BLOCK)
            q, do = b["qs"][s, few].reshape(BLOCK, LANES), b["datt"][s, few].reshape(BLOCK, LANES)
            at = jnp.concatenate(
                [column(row[:, j * PART : (j + 1) * PART]) for j in range(few.start, few.stop)], axis=0
            )
            allowed = keys_at <= at
            out = jnp.zeros((BLOCK, LANES), F32)
            dq = jnp.zeros((BLOCK, LANES), F32)
            for h in range(2):
                m = lane // HD == h
                qh, doh = jnp.where(m, q, zero), jnp.where(m, do, zero)
                score = jnp.where(allowed, mul(qh, k, 1, 1) * SCALE, -1e30)
                raised = jnp.exp(score - jnp.max(score, axis=1, keepdims=True))
                p = raised * (1.0 / jnp.sum(raised, axis=1, keepdims=True))
                p_low = p.astype(BF)
                oh = jnp.where(m, mul(p_low, v), 0.0)
                out = out + oh
                delta = jnp.sum(doh.astype(F32) * oh, axis=1, keepdims=True)
                ds = (p * (mul(doh, v, 1, 1) - delta)).astype(BF)
                dq = jnp.where(m, mul(ds, k), dq)
                dkh, dvh = mul(qh, ds, 0, 0), mul(doh, p_low, 0, 0)
                dk, dv = (dkh, dvh) if dk is None else (dk + dkh, dv + dvh)
            b["att"][s, at_rows] = out.astype(BF)
            cosine, sine = angles(tab[s, few].reshape(BLOCK, LANES))
            dq = turn(dq * SCALE, cosine, -sine)
            small[5:6, :LANES] += colsum(dq)
            b["dproj"][s, at_rows, :LANES] = dq.astype(BF)
        for n, v in enumerate((dk * SCALE, dv)):
            b["dkv_own"][s, n] = v[:, :HALF]
            b["dkv_out"][s, n] = v[:, HALF:].astype(BF)

    def branches(p, c):
        s = 2 * c + p
        v = mul(b["att"][s], wo[...]) + mul(b["hid"][s].reshape(HALF, HID), wr[...])
        b["ob"][p, c] = v.astype(BF).reshape(RING, PART, D)

    def combine(ref, at, half, p):
        @pl.loop(0, RING)
        def _(i):
            ref[(*at, i)] = (ref[(*at, i)].astype(F32) + half[p, i].astype(F32)).astype(BF)

    def spread(ref, at, ring, p):
        return [push(ref.at[(*at, (x + d) % 4)], ring.at[p, d - 1], xp[d - 1]) for d in (1, 3, 2)]

    dc, oc, oring = [], [], []
    for p in range(2):

        @pl.loop(0, 2)
        def _(c):
            attend(2 * c + p)

        dc.append([push(b["dkv_out"].at[s], b["dkv_in"].at[s], yp[1]) for s in (p, 2 + p)])

        if p == 1:
            oc[0].wait_recv()
            combine(b["ob"], (0, core), b["half"], 0)
            oring.append(spread(b["ob"], (0, core), b["ring_o"], 0))

        @pl.loop(0, 2)
        def _(c):
            branches(p, c)

        oc.append(push(b["ob"].at[p, 1 - core], b["half"].at[p], sib))

    rows = SEQ * HALF
    for k in range(2):
        two = slice(2 * k * LANES, 2 * (k + 1) * LANES)
        r = mul(b["hid"][..., two].reshape(rows, 2 * LANES), gs[...].reshape(rows, D), 0, 0).reshape(2, 16, OWN, D)
        for j in range(16):
            wrs[j // 4, j % 4, 2 * k * OWN : 2 * (k + 1) * OWN] = r[:, j].reshape(2 * OWN, D).astype(BF)
    o = mul(b["att"][...].reshape(rows, LANES), gs[...].reshape(rows, D), 0, 0)
    for j in range(16):
        wos[j // 4, j % 4] = fold(o[j * OWN : (j + 1) * OWN])
    rz = []
    for d in (1, 3, 2):
        ob = (bz + d) % 4
        rz.append(push(wrs.at[:, ob], b["rg_z"].at[d - 1], zp[d - 1]))
        rz.append(push(wos.at[:, ob], b["og_z"].at[d - 1], zp[d - 1]))
    oc[1].wait_recv()
    combine(b["ob"], (1, core), b["half"], 1)
    oring.append(spread(b["ob"], (1, core), b["ring_o"], 1))

    def inward(s):
        for n in range(2):
            v = (b["dkv_own"][s, n] + b["dkv_in"][s, n].astype(F32)).T
            if n == 0:
                cosine, sine = angles(tab[s].reshape(HALF, LANES))
                v = turn(v, cosine, -sine)
            small[5:6, (n + 1) * LANES : (n + 2) * LANES] += colsum(v)
            b["dproj"][s, :, (n + 1) * LANES : (n + 2) * LANES] = v.astype(BF)

        @pl.loop(0, 2)
        def _(i):
            two = pl.ds(2 * i, 2)
            rows = 2 * PART
            da = mul(
                b["dproj"][s, pl.ds(pl.multiple_of(i * rows, rows), rows)],
                wpe[:, :, :, :, :, 0:QKV].reshape(D, QKV), 1, 1,
            )
            db = mul(
                b["dexp"][s, two].reshape(rows, HID), wpe[:, :, :, :, :, QKV:].reshape(D, HID), 1, 1
            )
            st = tab[s, two].reshape(rows, LANES)
            n = (xs[s, two].reshape(rows, D).astype(F32) - st[:, ROT : ROT + 1]) * st[:, HD + ROT : HD + ROT + 1]
            small[0:1] += colsum(da * n)
            small[1:2] += colsum(da)
            small[2:3] += colsum(db * n)
            small[3:4] += colsum(db)
            xs[s, two] = (da * g1[...] + db * g2[...]).astype(BF).reshape(2, PART, D)

    def weight_grad(into, back_ref, to):
        for i in range(4):
            v = into[..., i * 2 * LANES : (i + 1) * 2 * LANES].reshape(rows, 2 * LANES)
            back = back_ref[...].reshape(rows, back_ref.shape[-1])
            e = mul(v, back, 0, 0).astype(BF).reshape(2, 2, 2, 4 * OWN, back.shape[1])
            to[i // 2, 2 * (i % 2) : 2 * (i % 2) + 2] = e

    hc, hring = [], []
    for p in range(2):
        for c in dc[p]:
            c.wait_recv()

        @pl.loop(0, 2)
        def _(c):
            inward(2 * c + p)

        hc.append(push(xs.at[2 * (1 - core) + p], b["half"].at[p], sib))
        if p == 0:
            weight_grad(second, b["dexp"], b["eg"])
            ez = [
                push(b["eg"].at[:, (z + d) % 4], b["eg_z"].at[d - 1], zp[d - 1]) for d in (1, 3, 2)
            ]
        hc[p].wait_recv()
        combine(xs, (2 * core + p,), b["half"], p)
        hring.append(spread(xs, (2 * core + p,), b["ring_h"], p))

    sz = [push(small, b["small_in"].at[d - 1], zp[d - 1]) for d in (1, 2, 3)]
    weight_grad(first, b["dproj"], b["pg"])
    pz = [push(b["pg"].at[:, (z + d) % 4], b["pg_z"].at[d - 1], zp[d - 1]) for d in (1, 3, 2)]

    def total(first_term, inbox):
        return (
            first_term.astype(F32) + inbox[0].astype(F32) + inbox[1].astype(F32) + inbox[2].astype(F32)
        )

    for c in rz:
        c.wait_recv()
    b["rg_b"][...] = total(wrs[:, bz], b["rg_z"]).astype(BF)
    b["og_b"][...] = total(wos[:, bz], b["og_z"]).astype(BF)
    ry = []
    for d in (1, 3, 2):
        to = (y + d) % 4
        ry.append(push(b["rg_b"].at[to], b["rg_y"].at[d - 1], yp[d - 1]))
        ry.append(push(b["og_b"].at[to], b["og_y"].at[d - 1], yp[d - 1]))

    def along_y(name, arrived):
        for c in arrived:
            c.wait_recv()
        b[name + "_b"][...] = total(b[name][:, z], b[name + "_z"]).astype(BF)
        out = []
        for d in (1, 3, 2):
            to = (y + d) % 4
            out.append(push(b[name + "_b"].at[to % 2, :, to // 2], b[name + "_y"].at[d - 1], yp[d - 1]))
        return out

    def to_owners(name, arrived):
        for c in arrived:
            c.wait_recv()
        width = b[name + "_f"].shape[-1]
        v = total(b[name + "_b"][ylo, :, yhi], b[name + "_y"])
        b[name + "_f"][...] = v.reshape(2, 4, OWN, width)
        b[name + "_all"][t] = b[name + "_f"][core, x]
        return [
            push(b[name + "_f"].at[uc, ux], b[name + "_all"].at[t], other) for ux, uc, other in group
        ]

    ey = along_y("eg", ez)
    for c in sz:
        c.wait_recv()
    b["small_b"][...] = small[...] + b["small_in"][0] + b["small_in"][1] + b["small_in"][2]
    sy = [push(b["small_b"], b["small_in"].at[2 + d], yp[d - 1]) for d in (1, 2, 3)]
    for c in ry:
        c.wait_recv()
    b["rg_f"][...] = total(b["rg_b"][y], b["rg_y"])
    b["og_f"][...] = unfold(total(b["og_b"][y], b["og_y"]))
    source = row_source(*me)
    back = [push(b["rg_f"], b["rg_all"], source), push(b["og_f"], owg_ref, source)]
    eo = to_owners("eg", ey)
    for c in sy:
        c.wait_recv()
    b["small_g"][...] = (
        b["small_b"][...] + b["small_in"][3] + b["small_in"][4] + b["small_in"][5]
    )
    b["small_all"][t] = b["small_g"][...]
    so = [push(b["small_g"], b["small_all"].at[t], other) for _, _, other in group]
    py = along_y("pg", pz)
    for p in range(2):
        for c in oring[p]:
            c.wait_recv()
        v = total(b["ob"][p, core, x], b["ring_o"].at[p])
        out_ref[p] = (x_ref[p].astype(F32) + v + bo_ref[...] + br_ref[...]).astype(BF)
    po = to_owners("pg", py)
    for c in back:
        c.wait_recv()
    r = b["rg_all"][...].reshape(GROUPS, OWN, D)
    for k in range(GROUPS):
        rwg_ref[:, k, :] = r[k]
    for c in eo:
        c.wait_recv()
    for u in range(TP):
        for k in range(GROUPS):
            ewg_ref[:, k * D + u * LANES : k * D + (u + 1) * LANES] = b["eg_all"][u, :, k * LANES : (k + 1) * LANES]
    for c in so:
        c.wait_recv()
    whole_ref[...] = sum(b["small_all"][u] for u in range(TP))
    for u in range(TP):
        for k in range(7):
            table_ref[0:1, k * D + u * LANES : k * D + (u + 1) * LANES] = b["small_all"][
                u, 5:6, k * LANES : (k + 1) * LANES
            ]
    for p in range(2):
        for c in hring[p]:
            c.wait_recv()
        h = total(xs[2 * core + p, x], b["ring_h"].at[p])
        st = tab[2 * core + p, x]
        r = st[:, HD + ROT : HD + ROT + 1]
        n = (x_ref[p].astype(F32) - st[:, ROT : ROT + 1]) * r
        inner = (
            h - jnp.mean(h, axis=1, keepdims=True) - n * jnp.mean(h * n, axis=1, keepdims=True)
        )
        dx_ref[p] = (g_ref[p].astype(F32) + r * inner).astype(BF)
    for c in po:
        c.wait_recv()
    for u in range(TP):
        for m in range(3):
            pwg_ref[:, m * D + u * LANES : m * D + (u + 1) * LANES] = b["pg_all"][u, :, m * LANES : (m + 1) * LANES]
    for c in wire.copies:
        if not any(c is w for w in settled):
            c.wait_send()


def shards(
    inputs, positions, first_gain, first_shift, second_gain, second_shift, project_weight,
    project_bias, output_weight, output_bias, expand_weight, expand_bias, reduce_weight,
    reduce_bias, cotangent,
):
    inverse = 10000.0 ** (-(np.arange(ROT // 2, dtype=np.float32) * 2.0 / ROT))
    by_lane = np.zeros((2, HD), np.float32)
    by_lane[:, :ROT] = np.concatenate([inverse, inverse]).astype(np.float32)
    line = lambda v: v.reshape(1, -1)
    shape = jax.ShapeDtypeStruct
    out, dx, pwg, owg, ewg, rwg, whole, table = pl.pallas_call(
        block_kernel,
        name="block",
        out_shape=(
            shape((2, PART, D), BF),
            shape((2, PART, D), BF),
            shape((OWN, 3 * D), F32),
            shape((OWN, D), F32),
            shape((OWN, FF), F32),
            shape((OWN, GROUPS, D), F32),
            shape((8, D), F32),
            shape((1, 7 * D), F32),
        ),
        in_specs=[VMEM] * 16,
        out_specs=(VMEM,) * 8,
        scratch_shapes=[pltpu.VMEM(*v) for v in SCRATCH.values()]
        + [pltpu.SemaphoreType.DMA((COPIES,)), pltpu.SemaphoreType.DMA((COPIES,))],
        compiler_params=pltpu.CompilerParams(
            collective_id=0, has_side_effects=True, vmem_limit_bytes=64 * 2**20
        ),
    )(
        inputs, cotangent, positions, jnp.asarray(by_lane.reshape(1, LANES)),
        line(first_gain), line(first_shift), line(second_gain), line(second_shift),
        project_weight, line(project_bias), output_weight, line(output_bias),
        expand_weight, line(expand_bias), reduce_weight, line(reduce_bias),
    )
    index = lax.axis_index("dp") * 8 + lax.axis_index("ctx")
    vec = lax.dynamic_slice_in_dim(whole, index * 8, 8, 1)
    bpg = lax.dynamic_slice_in_dim(table[0, : 3 * D], index * 24, 24, 0)
    beg = lax.dynamic_slice_in_dim(table[0, 3 * D :], index * 32, 32, 0)
    return (
        out, dx, vec[0], vec[1], vec[2], vec[3], pwg, bpg, owg, vec[4], ewg, beg, rwg, vec[4],
    )


def solution(mesh):
    rows = P(("dp", "ctx"), None)
    vector = P(("dp", "ctx"))
    tokens = P("dp", "ctx", None)
    deep = P(("dp", "ctx"), None, None)
    return jax.shard_map(
        shards,
        mesh=mesh,
        in_specs=(
            tokens, P("dp", None), P(), P(), P(), P(), rows, P(), rows, P(), rows, P(), deep, P(),
            tokens,
        ),
        out_specs=(
            tokens, tokens, vector, vector, vector, vector, rows, vector, rows, vector, rows,
            vector, deep, vector,
        ),
        check_vma=False,
    )
```

```python
import jax
import jax.numpy as jnp
import numpy as np
from jax import lax
from jax.experimental import pallas as pl
from jax.experimental.pallas import tpu as pltpu
from jax.sharding import PartitionSpec as P

D = 1024
HD = 64
ROT = 16
FF = 4096
GROUPS = 4
EPSILON = 1e-05

RING = 4
TP = 8
SEQ = 4
PART = 128
STRETCH = 64
HALF = RING * PART
FULL = 2 * HALF
OWN = 8
LANES = 128
QKV = 3 * LANES
HID = GROUPS * LANES
WIDE = QKV + HID
SCALE = HD ** (-0.5)
BLOCK = 256

MESH = pl.DeviceIdType.MESH
VMEM = pl.BlockSpec(memory_space=pltpu.VMEM)
BF = jnp.bfloat16
F32 = jnp.float32


def place():
    dp, ctx = lax.axis_index("dp"), lax.axis_index("ctx")
    return ctx % 4, (ctx // 4) * 2 + dp // 8, (dp // 2) % 4, dp % 2


def device(x, y, z, core):
    return {"dp": ((y % 2) * 4 + z) * 2 + core, "ctx": (y // 2) * 4 + x}


class Copy:
    def __init__(self, copy):
        self.copy, self.left, self.here = copy, False, False

    def wait_send(self):
        if not self.left:
            self.left = True
            self.copy.wait_send()

    def wait_recv(self):
        if not self.here:
            self.here = True
            self.copy.wait_recv()


class Wire:
    def __init__(self, send, recv):
        self.send, self.recv, self.copies = send, recv, []

    def push(self, src, dst, to):
        i = len(self.copies)
        copy = pltpu.make_async_remote_copy(
            src_ref=src,
            dst_ref=dst,
            send_sem=self.send.at[i],
            recv_sem=self.recv.at[i],
            device_id=to,
            device_id_type=MESH,
        )
        copy.start()
        self.copies.append(Copy(copy))
        return self.copies[-1]


def arrive(copies):
    for c in copies:
        c.wait_recv()


def row_owner(x, y, z, core):
    ylo = y % 2
    return device(ylo * 2 + z // 2, core * 2 + y // 2, (x + 3 + 2 * ylo) % 4, z % 2)


def row_source(x, y, z, core):
    ylo = x // 2
    return device((z + 1 + 2 * ylo) % 4, (y % 2) * 2 + ylo, (x % 2) * 2 + core, y // 2)


def row_block(x, y, z):
    return y, (z + 1 + 2 * (x // 2)) % 4


def fold(rows):
    return jnp.concatenate([rows[:, : D // 2], rows[:, D // 2 :]], axis=0).astype(BF)


def unfold(rows):
    return jnp.concatenate([rows[:OWN], rows[OWN:]], axis=1)


def mul(a, b, ca=1, cb=0):
    return lax.dot_general(a, b, (((ca,), (cb,)), ((), ())), preferred_element_type=F32)


def lane_of(rows):
    return lax.broadcasted_iota(jnp.int32, (rows, LANES), 1)


def turn(v, cosine, sine):
    low = lane_of(v.shape[0]) % HD < ROT // 2
    mate = jnp.where(low, pltpu.roll(v, LANES - ROT // 2, 1), pltpu.roll(v, ROT // 2, 1))
    return v * cosine + mate * sine


def column(row):
    r = lax.broadcasted_iota(jnp.int32, (PART, 1), 0)
    base = jnp.where(r < STRETCH, row[:, 0:1], row[:, STRETCH : STRETCH + 1])
    return base + (r % STRETCH).astype(F32)


def colsum(v):
    return jnp.sum(v, axis=0, keepdims=True)


SCRATCH = dict(
    pe_s=((TP, 2 * OWN, D // 2), BF),
    stage=((2, 4, 2 * OWN, D // 2), BF),
    wp=((2, 4, 2, 2, 4 * OWN, QKV), BF),
    we=((2, 4, 2, 2, 4 * OWN, HID), BF),
    wo_own=((2 * OWN, D // 2), BF),
    wr_f=((GROUPS, OWN, D), F32),
    wr_own=((GROUPS * OWN, D), BF),
    wos=((4, 4, 2 * OWN, D // 2), BF),
    wrs=((4, 4, GROUPS * OWN, D), BF),
    wo=((LANES, D), BF),
    wr=((HID, D), BF),
    xs=((SEQ, RING, PART, D), BF),
    gs=((SEQ, RING, PART, D), BF),
    ps=((2, 8, FULL), F32),
    first=((SEQ, RING, PART, D), BF),
    second=((SEQ, RING, PART, D), BF),
    tab=((SEQ, RING, PART, LANES), F32),
    qs=((SEQ, RING, PART, LANES), BF),
    kv=((2, SEQ, 2, RING, PART, LANES), BF),
    att=((SEQ, HALF, LANES), BF),
    hid=((SEQ, RING, PART, HID), BF),
    dexp=((SEQ, RING, PART, HID), BF),
    datt=((SEQ, RING, PART, LANES), BF),
    dkv_own=((SEQ, 2, LANES, HALF), F32),
    dkv_out=((SEQ, 2, LANES, HALF), BF),
    dkv_in=((SEQ, 2, LANES, HALF), BF),
    dproj=((SEQ, HALF, QKV), BF),
    ob=((2, 2, RING, PART, D), BF),
    half=((2, RING, PART, D), BF),
    via_o=((2, 2, PART // 2, D), BF),
    via_h=((2, 2, PART // 2, D), BF),
    ring_o=((2, 2, PART, D), BF),
    ring_h=((2, 2, PART, D), BF),
    small=((8, D), F32),
    small_in=((6, 8, D), F32),
    small_b=((8, D), F32),
    small_g=((8, D), F32),
    small_all=((TP, 8, D), F32),
    rg_a=((3, 4, 2 * OWN, D), BF),
    rg_b=((3, 4, 2 * OWN, D), BF),
    rg_m=((2, 4, 2 * OWN, D), BF),
    rg_n=((2, 3, 2 * OWN, D), BF),
    rg_f=((GROUPS * OWN, D), F32),
    rg_all=((GROUPS * OWN, D), F32),
    og_a=((3, 4, 2 * OWN, D // 2), BF),
    og_m=((4, 2 * OWN, D // 2), BF),
    og_n=((3, 2 * OWN, D // 2), BF),
    og_f=((OWN, D), F32),
    eg=((2, 4, 2, 2, 4 * OWN, HID), BF),
    eg_a=((3, 2, 2, 4 * OWN, HID), BF),
    eg_b=((3, 4, 4 * OWN, HID), BF),
    eg_m=((2, 2, 4 * OWN, HID), BF),
    eg_k=((4, 4 * OWN, HID), BF),
    eg_n=((2, 3, 4 * OWN, HID), BF),
    eg_f=((2, 4, OWN, HID), F32),
    eg_all=((TP, OWN, HID), F32),
    pg=((2, 4, 2, 2, 4 * OWN, QKV), BF),
    pg_a=((3, 2, 2, 4 * OWN, QKV), BF),
    pg_b=((3, 4, 4 * OWN, QKV), BF),
    pg_m=((2, 2, 4 * OWN, QKV), BF),
    pg_k=((4, 4 * OWN, QKV), BF),
    pg_n=((2, 3, 4 * OWN, QKV), BF),
    pg_f=((2, 4, OWN, QKV), F32),
    pg_all=((TP, OWN, QKV), F32),
)
COPIES = 192


def block_kernel(
    x_ref, g_ref, pos_ref, inv_ref, cos_in, sin_in, g1, s1, g2, s2, pw_ref, bp_ref, ow_ref, bo_ref, ew_ref, be_ref,
    rw_ref, br_ref,
    out_ref, dx_ref, pwg_ref, owg_ref, ewg_ref, rwg_ref, whole_ref, table_ref,
    *scratch,
):
    b = dict(zip(SCRATCH, scratch))
    send, recv = scratch[len(SCRATCH) :]
    xs, gs, ps, first, second, tab = (b[n] for n in ("xs", "gs", "ps", "first", "second", "tab"))
    wp, we, wos, wrs, wo, wr, kv = (b[n] for n in ("wp", "we", "wos", "wrs", "wo", "wr", "kv"))
    small = b["small"]
    x, y, z, core = place()
    me = (x, y, z, core)
    t = x * 2 + core
    ylo, yhi = y % 2, y // 2
    sib = device(x, y, z, 1 - core)
    xp = [device((x + d) % 4, y, z, core) for d in (1, 2, 3)]
    xq = [device((x + d) % 4, y, z, 1 - core) for d in (1, 2, 3)]
    yp = [device(x, (y + d) % 4, z, core) for d in (1, 2, 3)]
    zp = [device(x, y, (z + d) % 4, core) for d in (1, 2, 3)]
    mine = pl.ds(2 * core, 2)
    group = [(x, 1 - core, sib)]
    group += [((x + d) % 4, core, xp[d - 1]) for d in (1, 2, 3)]
    group += [((x + d) % 4, 1 - core, xq[d - 1]) for d in (1, 2, 3)]
    t128 = pl.multiple_of(t * LANES, LANES)

    senders = xp + [sib] + xq + yp + zp + [row_source(*me), row_owner(*me)]
    barrier = pltpu.get_barrier_semaphore()
    for other in senders:
        pl.semaphore_signal(barrier, inc=1, device_id=other, device_id_type=MESH)

    pw, ew = pw_ref[...].astype(F32), ew_ref[...].astype(F32)
    for u in range(TP):
        at = slice(u * LANES, (u + 1) * LANES)
        parts = [pw[:, m * D : (m + 1) * D][:, at] for m in range(3)]
        parts += [ew[:, k * D : (k + 1) * D][:, at] for k in range(GROUPS)]
        b["pe_s"][u] = fold(jnp.concatenate(parts + [jnp.zeros((OWN, LANES), F32)], axis=1))
    xs[mine, x] = x_ref[...]
    pl.semaphore_wait(barrier, len(senders))
    wire = Wire(send, recv)
    push = wire.push

    def to_neighbours(buf):
        a, c, both = buf.at[2 * core, x], buf.at[2 * core + 1, x], buf.at[mine, x]
        ahead = push(a, a, xp[0])
        back = push(c, c, xp[2])
        return [ahead, back, push(both, both, sib), push(c, c, xp[0]), push(a, a, xp[2])]

    step = [push(b["pe_s"].at[ux * 2 + uc], b["stage"].at[core, x], other) for ux, uc, other in group]
    b["stage"][core, x] = b["pe_s"][t]
    b["wo_own"][...] = fold(ow_ref[...].astype(F32))
    for i in range(OWN):
        b["wr_f"][:, i, :] = rw_ref[i].astype(F32)
    b["wr_own"][...] = b["wr_f"][...].reshape(GROUPS * OWN, D).astype(BF)
    by, bz = row_block(*me[:3])
    owner = row_owner(*me)
    oy, oz = core * 2 + yhi, x
    step_rows = [
        push(b["wo_own"], wos.at[oy, oz], owner),
        push(b["wr_own"], wrs.at[oy, oz], owner),
    ]
    xc = to_neighbours(xs)
    ps[core] = jnp.zeros((8, FULL), F32)
    ps[core, 0:2] = pos_ref[...].astype(F32)
    sp = push(ps.at[core], ps.at[core], sib)
    gs[mine, x] = g_ref[...]
    small[...] = jnp.zeros_like(small)
    tab[...] = jnp.zeros_like(tab)

    def keep_turn(s, j, v, turning):
        tab[s, j] = jnp.where((lane_of(PART) % HD < ROT) == turning, v, tab[s, j])

    def angles(v):
        lane, back = lane_of(v.shape[0]), pltpu.roll(v, HD, 1)
        turned = lane % HD < ROT
        cosine = jnp.where(turned, jnp.where(lane < HD, v, back), 1.0)
        return cosine, jnp.where(turned, jnp.where(lane < HD, back, v), 0.0)

    def layer_norm(s0, count, j):
        @pl.loop(0, count)
        def _(i):
            s = s0 + i
            v = xs[s, j].astype(F32)
            mean = jnp.mean(v, axis=1, keepdims=True)
            c = v - mean
            r = lax.rsqrt(jnp.mean(c * c, axis=1, keepdims=True) + EPSILON)
            n = c * r
            first[s, j] = (n * g1[...] + s1[...]).astype(BF)
            second[s, j] = (n * g2[...] + s2[...]).astype(BF)
            keep_turn(s, j, jnp.where(lane_of(PART) < HD, mean, r), False)

    def tables():
        firsts = []
        for s in range(SEQ):
            row = ps[s // 2, s % 2 : s % 2 + 1, pl.ds(pl.multiple_of(yhi * HALF, HALF), HALF)]
            firsts += [row[:, i * STRETCH : i * STRETCH + 1] for i in range(2 * RING)]
        angle = jnp.concatenate(firsts, axis=0) * inv_ref[...]
        cosine, sine = jnp.cos(angle), jnp.sin(angle)
        lane = lane_of(STRETCH)
        sign = jnp.where(lane % HD < ROT // 2, -1.0, 1.0)
        for s in range(SEQ):
            for j in range(RING):
                two = []
                for i in range(2):
                    n = (s * RING + j) * 2 + i
                    c, v = cosine[n : n + 1], sine[n : n + 1]
                    both = jnp.where(
                        lane < HD,
                        c * cos_in[...] - v * sin_in[...],
                        (v * cos_in[...] + c * sin_in[...]) * sign,
                    )
                    two.append(both)
                keep_turn(s, j, jnp.concatenate(two, axis=0), True)

    bias_p = jnp.concatenate([bp_ref[:, pl.ds(pl.multiple_of(m * D + t128, LANES), LANES)] for m in range(3)], axis=1)
    bias_e = jnp.concatenate(
        [be_ref[:, pl.ds(pl.multiple_of(k * D + t128, LANES), LANES)] for k in range(GROUPS)], axis=1
    )

    def project(j):
        p = mul(first[:, j].reshape(HALF, D), wp[...].reshape(D, QKV)) + bias_p
        c, s = angles(tab[:, j].reshape(HALF, LANES))
        shape = (SEQ, PART, LANES)
        b["qs"][:, j] = turn(p[:, :LANES], c, s).astype(BF).reshape(shape)
        kv[0, :, 0, j] = turn(p[:, LANES : 2 * LANES], c, s).astype(BF).reshape(shape)
        kv[1, :, 0, j] = p[:, 2 * LANES :].astype(BF).reshape(shape)
        return push(kv.at[:, :, 0, j], kv.at[:, :, 1, j], yp[1])

    def expand(j):
        e = mul(second[:, j].reshape(HALF, D), we[...].reshape(D, HID)) + bias_e
        cdf = 0.5 * (1.0 + lax.erf(e * 0.5**0.5))
        b["hid"][:, j] = (e * cdf).astype(BF).reshape(SEQ, PART, HID)
        slope = cdf + e * (jnp.exp(-0.5 * e * e) * (2.0 * np.pi) ** -0.5)
        b["dexp"][:, j] = slope.astype(BF).reshape(SEQ, PART, HID)

    def across_y(buf):
        out = []
        for d in (0, 2, 1):
            v = buf.at[ylo, z, 0, yhi]
            out.append(push(v, v, yp[d]))
            v = buf.at[ylo, z, 1, yhi]
            out.append(push(v, v, zp[d]))
        return out

    def across_z(buf):
        out = []
        for d in (0, 2, 1):
            v = buf.at[:, z, 0]
            out.append(push(v, v, zp[d]))
            v = buf.at[ylo, :, 1, yhi]
            out.append(push(v, v, yp[d]))
        return out

    def across_y(buf):
        out = []
        for d in (0, 2, 1):
            v = buf.at[ylo, z, 0, yhi]
            out.append(push(v, v, yp[d]))
            v = buf.at[ylo, z, 1, yhi]
            out.append(push(v, v, zp[d]))
        return out

    def across_z(buf):
        out = []
        for d in (0, 2, 1):
            v = buf.at[:, z, 0]
            out.append(push(v, v, zp[d]))
            v = buf.at[ylo, :, 1, yhi]
            out.append(push(v, v, yp[d]))
        return out

    def along_y(v):
        return [push(v, v, yp[d]) for d in (0, 2, 1)]

    def near_z(v):
        return [push(v, v, zp[0]), push(v, v, zp[2])]

    def far_z(came, ahead, back):
        came[0].wait_recv()
        out = [push(ahead, ahead, zp[0])]
        came[1].wait_recv()
        return out + [push(back, back, zp[2])]

    layer_norm(2 * core, 2, x)
    xc[2].wait_recv()
    layer_norm(2 - 2 * core, 2, x)
    sp.wait_recv()
    tables()
    arrive(step)
    for c in range(2):
        v = [unfold(b["stage"][c, i].astype(F32)) for i in range(4)]
        v = jnp.concatenate(v, axis=0).astype(BF)
        wp[ylo, z, c, yhi] = v[:, :QKV]
        we[ylo, z, c, yhi] = v[:, QKV:WIDE]
    p1 = across_y(wp)
    e1 = along_y(we.at[ylo, z, :, yhi])
    arrive(step_rows)
    o1 = along_y(wos.at[by, bz])
    w1 = along_y(wrs.at[by, bz])
    arrive(p1)
    p2 = across_z(wp)
    top, low = pl.ds(0, 2 * OWN), pl.ds(2 * OWN, 2 * OWN)
    before, after, far = (x + 3) % 4, (x + 1) % 4, (x + 2) % 4

    def relay(buf, near):
        near[0].wait_recv()
        v = buf.at[2 * core, before]
        ahead = push(v, v, xp[0])
        near[1].wait_recv()
        v = buf.at[2 * core + 1, after]
        back = push(v, v, xp[2])
        return [ahead, back]

    def relay_core(buf, near):
        v, w = buf.at[mine, before], buf.at[mine, after]
        near[3].wait_recv()
        out = [push(v, v, sib)]
        near[4].wait_recv()
        return out + [push(w, w, sib)]

    def relay_far(buf, fars):
        fars[0].wait_recv()
        v = buf.at[2 * core, far]
        a = push(v, v, sib)
        fars[1].wait_recv()
        w = buf.at[2 * core + 1, far]
        return [a, push(w, w, sib)]

    xf = relay(xs, xc)
    xd = relay_core(xs, xc)
    gc = to_neighbours(gs)
    layer_norm(2 * core, 2, before)
    layer_norm(2 * core, 2, after)
    arrive(p2)
    kc = [project(x)]
    arrive(e1)
    e2 = near_z(we.at[:, z])
    arrive(o1)
    o2 = []
    for d in (0, 2, 1):
        v = wos.at[:, bz]
        o2.append(push(v, v, zp[d]))
    arrive(xd)
    layer_norm(2 - 2 * core, 2, before)
    kc.append(project(before))
    xfd = relay_far(xs, xf)
    layer_norm(2 - 2 * core, 2, after)
    kc.append(project(after))
    e3 = far_z(e2, we.at[:, (z + 3) % 4, 0], we.at[:, (z + 1) % 4, 1])
    arrive(w1)
    w2 = near_z(wrs.at[:, bz])
    layer_norm(2 * core, 2, far)
    arrive(xfd)
    layer_norm(2 - 2 * core, 2, far)
    kc.append(project(far))
    arrive(e3)
    expand(x)
    gf = relay(gs, gc)
    gd = relay_core(gs, gc)
    w3 = far_z(w2, wrs.at[:, (bz + 3) % 4, top], wrs.at[:, (bz + 1) % 4, low])
    expand(before)
    arrive(o2)
    for i in range(8):
        two = [unfold(wos[2 * i // 4, 2 * i % 4 + n].astype(F32)) for n in range(2)]
        wo[2 * i * OWN : 2 * (i + 1) * OWN] = jnp.concatenate(two, axis=0).astype(BF)
    expand(after)
    gfd = relay_far(gs, gf)
    expand(far)

    arrive(w3)
    wr_all = wrs[...].reshape(16, GROUPS, OWN, D).astype(F32)
    for k in range(GROUPS):
        wr[k * LANES : (k + 1) * LANES] = wr_all[:, k].reshape(LANES, D).astype(BF)

    small[4:5] = colsum(g_ref[...].astype(F32).reshape(2 * PART, D))

    def back_attention(j):
        g = gs[:, j].reshape(HALF, D)
        b["datt"][:, j] = mul(g, wo[...], 1, 1).astype(BF).reshape(SEQ, PART, LANES)

    def back_hidden(j):
        g = gs[:, j].reshape(HALF, D)
        d = mul(g, wr[...], 1, 1) * b["dexp"][:, j].reshape(HALF, HID).astype(F32)
        small[5:6, QKV:WIDE] += colsum(d)
        b["dexp"][:, j] = d.astype(BF).reshape(SEQ, PART, HID)

    gc[2].wait_recv()
    back_attention(x)
    back_hidden(x)
    arrive(gd)
    back_attention(before)
    back_attention(after)
    back_hidden(before)
    arrive(gfd)
    back_attention(far)
    for c in xc + xf + xd + xfd + step_rows + o1 + o2 + w1 + w2 + w3:
        c.wait_send()
    arrive(kc)

    def attend(s):
        k, v = kv[0, s].reshape(FULL, LANES), kv[1, s].reshape(FULL, LANES)
        row = ps[s // 2, pl.ds(s % 2, 1), pl.ds(pl.multiple_of(yhi * HALF, HALF), HALF)]
        other = ps[s // 2, pl.ds(s % 2, 1), pl.ds(pl.multiple_of((1 - yhi) * HALF, HALF), HALF)]
        keys_at = jnp.concatenate([row, other], axis=1)
        lane = lane_of(BLOCK)
        zero = jnp.zeros((BLOCK, LANES), BF)
        dk = dv = None
        for i in range(HALF // BLOCK):
            few = slice(i * BLOCK // PART, (i + 1) * BLOCK // PART)
            at_rows = slice(i * BLOCK, (i + 1) * BLOCK)
            q, do = b["qs"][s, few].reshape(BLOCK, LANES), b["datt"][s, few].reshape(BLOCK, LANES)
            at = jnp.concatenate(
                [column(row[:, j * PART : (j + 1) * PART]) for j in range(few.start, few.stop)], axis=0
            )
            allowed = keys_at <= at
            out = jnp.zeros((BLOCK, LANES), F32)
            dq = jnp.zeros((BLOCK, LANES), F32)
            for h in range(2):
                m = lane // HD == h
                qh, doh = jnp.where(m, q, zero), jnp.where(m, do, zero)
                score = jnp.where(allowed, mul(qh, k, 1, 1) * SCALE, -1e30)
                raised = jnp.exp(score - jnp.max(score, axis=1, keepdims=True))
                p = raised * (1.0 / jnp.sum(raised, axis=1, keepdims=True))
                p_low = p.astype(BF)
                oh = jnp.where(m, mul(p_low, v), 0.0)
                out = out + oh
                delta = jnp.sum(doh.astype(F32) * oh, axis=1, keepdims=True)
                ds = (p * (mul(doh, v, 1, 1) - delta)).astype(BF)
                dq = jnp.where(m, mul(ds, k), dq)
                dkh, dvh = mul(qh, ds, 0, 0), mul(doh, p_low, 0, 0)
                dk, dv = (dkh, dvh) if dk is None else (dk + dkh, dv + dvh)
            b["att"][s, at_rows] = out.astype(BF)
            cosine, sine = angles(tab[s, few].reshape(BLOCK, LANES))
            dq = turn(dq * SCALE, cosine, -sine)
            small[5:6, :LANES] += colsum(dq)
            b["dproj"][s, at_rows, :LANES] = dq.astype(BF)
        for n, v in enumerate((dk * SCALE, dv)):
            b["dkv_own"][s, n] = v[:, :HALF]
            b["dkv_out"][s, n] = v[:, HALF:].astype(BF)

    def branches(p, c):
        s = 2 * c + p
        v = mul(b["att"][s], wo[...]) + mul(b["hid"][s].reshape(HALF, HID), wr[...])
        b["ob"][p, c] = v.astype(BF).reshape(RING, PART, D)

    def combine(ref, at, half, p):
        @pl.loop(0, RING)
        def _(i):
            ref[(*at, i)] = (ref[(*at, i)].astype(F32) + half[p, i].astype(F32)).astype(BF)

    def far_block(ref, at, via, p):
        halves = ref.at[(*at, far, pl.ds(0, PART // 2))], ref.at[(*at, far, pl.ds(PART // 2, PART // 2))]
        return [push(v, via.at[p, i], xp[2 * i]) for i, v in enumerate(halves)]

    def near_blocks(ref, at, via, ring, p, came):
        out = []
        for i, to in enumerate((after, before)):
            came[i].wait_recv()
            where = (*at, to, pl.ds(i * PART // 2, PART // 2))
            ref[where] = (ref[where].astype(F32) + via[p, i].astype(F32)).astype(BF)
            v = ref.at[(*at, to)]
            out.append(push(v, ring.at[p, i], xp[2 * i]))
        return out

    rows = SEQ * HALF

    def weight_grad(into, back_ref, to):
        for i in range(4):
            v = into[..., i * 2 * LANES : (i + 1) * 2 * LANES].reshape(rows, 2 * LANES)
            back = back_ref[...].reshape(rows, back_ref.shape[-1])
            e = mul(v, back, 0, 0).astype(BF).reshape(2, 2, 2, 4 * OWN, back.shape[1])
            to[i // 2, 2 * (i % 2) : 2 * (i % 2) + 2] = e

    def plus(first_term, inbox):
        v = first_term.astype(F32)
        for i in range(inbox.shape[0]):
            v = v + inbox[i].astype(F32)
        return v

    def reduce_1(name):
        g = b[name]
        out = []
        for d in (1, 3, 2):
            out.append(push(g.at[:, (z + d) % 4, 0], b[name + "_a"].at[d - 1], zp[d - 1]))
            to = (y + d) % 4
            out.append(push(g.at[to % 2, :, 1, to // 2], b[name + "_b"].at[d - 1], yp[d - 1]))
        return out

    def reduce_2(name, came):
        arrive(came)
        g, m, k, n = b[name], b[name + "_m"], b[name + "_k"], b[name + "_n"]
        m[...] = plus(g[:, z, 0], b[name + "_a"]).astype(BF)
        k[...] = plus(g[ylo, :, 1, yhi], b[name + "_b"]).astype(BF)
        out = []
        for d in (1, 3, 2):
            to = (y + d) % 4
            out.append(push(m.at[to % 2, to // 2], n.at[0, d - 1], yp[d - 1]))
            out.append(push(k.at[(z + d) % 4], n.at[1, d - 1], zp[d - 1]))
        return out

    def to_owners(name, came):
        arrive(came)
        f, whole, n = b[name + "_f"], b[name + "_all"], b[name + "_n"]
        width = f.shape[-1]
        f[0] = plus(b[name + "_m"][ylo, yhi], n.at[0]).reshape(4, OWN, width)
        f[1] = plus(b[name + "_k"][z], n.at[1]).reshape(4, OWN, width)
        whole[t] = f[core, x]
        return [push(f.at[uc, ux], whole.at[t], other) for ux, uc, other in group]

    theirs, ours = 1 - core, core

    def pair(f, p):
        @pl.loop(0, 2)
        def _(c):
            f(2 * ((c + theirs) % 2) + p)

    ob, half = b["ob"], b["half"]
    pair(attend, 0)
    dc = [push(b["dkv_out"].at[s], b["dkv_in"].at[s], yp[1]) for s in (0, 2)]
    branches(0, theirs)
    oc = [push(ob.at[0, theirs], half.at[0], sib)]
    branches(0, ours)
    back_hidden(after)
    back_hidden(far)

    for k in range(2):
        two = slice(2 * k * LANES, 2 * (k + 1) * LANES)
        r = mul(b["hid"][..., two].reshape(rows, 2 * LANES), gs[...].reshape(rows, D), 0, 0)
        r = r.reshape(2, 16, OWN, D)
        for j in range(16):
            wrs[j // 4, j % 4, 2 * k * OWN : 2 * (k + 1) * OWN] = r[:, j].reshape(2 * OWN, D).astype(BF)
    rc = []
    for d in (1, 3, 2):
        rc.append(push(wrs.at[:, (bz + d) % 4, top], b["rg_a"].at[d - 1], zp[d - 1]))
        rc.append(push(wrs.at[(y + d) % 4, :, low], b["rg_b"].at[d - 1], yp[d - 1]))
    arrive(oc)
    combine(ob, (0, core), half, 0)
    ofar = [far_block(ob, (0, core), b["via_o"], 0)]

    attend(2 * theirs + 1)
    oring = [near_blocks(ob, (0, core), b["via_o"], b["ring_o"], 0, ofar[0])]
    attend(2 * ours + 1)
    dc += [push(b["dkv_out"].at[s], b["dkv_in"].at[s], yp[1]) for s in (1, 3)]
    branches(1, theirs)
    oc.append(push(ob.at[1, theirs], half.at[1], sib))
    branches(1, ours)

    o = mul(b["att"][...].reshape(rows, LANES), gs[...].reshape(rows, D), 0, 0)
    for j in range(16):
        wos[j // 4, j % 4] = fold(o[j * OWN : (j + 1) * OWN])
    arrive(rc)
    b["rg_m"][0] = plus(wrs[:, bz, top], b["rg_a"]).astype(BF)
    b["rg_m"][1] = plus(wrs[y, :, low], b["rg_b"]).astype(BF)
    r2 = []
    for d in (1, 3, 2):
        r2.append(push(b["rg_m"].at[0, (y + d) % 4], b["rg_n"].at[0, d - 1], yp[d - 1]))
        r2.append(push(b["rg_m"].at[1, (bz + d) % 4], b["rg_n"].at[1, d - 1], zp[d - 1]))
    og1 = [push(wos.at[:, (bz + d) % 4], b["og_a"].at[d - 1], zp[d - 1]) for d in (1, 3, 2)]
    arrive(oc)
    combine(ob, (1, core), half, 1)
    ofar.append(far_block(ob, (1, core), b["via_o"], 1))

    def inward(s):
        for n in range(2):
            v = (b["dkv_own"][s, n] + b["dkv_in"][s, n].astype(F32)).T
            if n == 0:
                cosine, sine = angles(tab[s].reshape(HALF, LANES))
                v = turn(v, cosine, -sine)
            small[5:6, (n + 1) * LANES : (n + 2) * LANES] += colsum(v)
            b["dproj"][s, :, (n + 1) * LANES : (n + 2) * LANES] = v.astype(BF)

        @pl.loop(0, 2)
        def _(i):
            two = pl.ds(2 * i, 2)
            some = 2 * PART
            da = mul(
                b["dproj"][s, pl.ds(pl.multiple_of(i * some, some), some)],
                wp[...].reshape(D, QKV), 1, 1,
            )
            db = mul(b["dexp"][s, two].reshape(some, HID), we[...].reshape(D, HID), 1, 1)
            st = tab[s, two].reshape(some, LANES)
            n = (xs[s, two].reshape(some, D).astype(F32) - st[:, ROT : ROT + 1]) * st[:, HD + ROT : HD + ROT + 1]
            small[0:1] += colsum(da * n)
            small[1:2] += colsum(da)
            small[2:3] += colsum(db * n)
            small[3:4] += colsum(db)
            xs[s, two] = (da * g1[...] + db * g2[...]).astype(BF).reshape(2, PART, D)

    arrive(dc[:2])
    inward(2 * theirs)
    hc = [push(xs.at[2 * theirs], half.at[0], sib)]
    oring.append(near_blocks(ob, (1, core), b["via_o"], b["ring_o"], 1, ofar[1]))
    inward(2 * ours)
    arrive(hc)
    combine(xs, (2 * core,), half, 0)
    hfar = [far_block(xs, (2 * core,), b["via_h"], 0)]
    weight_grad(second, b["dexp"], b["eg"])
    ec = reduce_1("eg")
    arrive(dc[2:])
    inward(2 * theirs + 1)
    hc.append(push(xs.at[2 * theirs + 1], half.at[1], sib))
    hring = [near_blocks(xs, (2 * core,), b["via_h"], b["ring_h"], 0, hfar[0])]
    inward(2 * ours + 1)

    sz = [push(small, b["small_in"].at[d - 1], zp[d - 1]) for d in (1, 2, 3)]
    arrive(hc)
    combine(xs, (2 * core + 1,), half, 1)
    hfar.append(far_block(xs, (2 * core + 1,), b["via_h"], 1))
    weight_grad(first, b["dproj"], b["pg"])
    pc = reduce_1("pg")
    hring.append(near_blocks(xs, (2 * core + 1,), b["via_h"], b["ring_h"], 1, hfar[1]))
    ec = reduce_2("eg", ec)
    arrive(og1)
    b["og_m"][...] = plus(wos[:, bz], b["og_a"]).astype(BF)
    og2 = [push(b["og_m"].at[(y + d) % 4], b["og_n"].at[d - 1], yp[d - 1]) for d in (1, 3, 2)]
    arrive(sz)
    b["small_b"][...] = plus(small[...], b["small_in"].at[pl.ds(0, 3)])
    sy = [push(b["small_b"], b["small_in"].at[2 + d], yp[d - 1]) for d in (1, 2, 3)]
    arrive(r2)
    b["rg_f"][top] = plus(b["rg_m"][0, y], b["rg_n"].at[0])
    b["rg_f"][low] = plus(b["rg_m"][1, bz], b["rg_n"].at[1])
    source = row_source(*me)
    back = [push(b["rg_f"], b["rg_all"], source)]
    pc = reduce_2("pg", pc)
    arrive(sy)
    b["small_g"][...] = plus(b["small_b"][...], b["small_in"].at[pl.ds(3, 3)])
    b["small_all"][t] = b["small_g"][...]
    so = [push(b["small_g"], b["small_all"].at[t], other) for _, _, other in group]
    arrive(og2)
    b["og_f"][...] = unfold(plus(b["og_m"][y], b["og_n"]))
    back.append(push(b["og_f"], owg_ref, source))
    eo = to_owners("eg", ec)
    for p in range(2):
        arrive(oring[p])
        v = plus(ob[p, core, x], b["ring_o"].at[p])
        out_ref[p] = (x_ref[p].astype(F32) + v + bo_ref[...] + br_ref[...]).astype(BF)
    po = to_owners("pg", pc)
    arrive(back)
    r = b["rg_all"][...].reshape(GROUPS, OWN, D)
    for k in range(GROUPS):
        rwg_ref[:, k, :] = r[k]
    arrive(eo)
    for u in range(TP):
        for k in range(GROUPS):
            ewg_ref[:, k * D + u * LANES : k * D + (u + 1) * LANES] = b["eg_all"][u, :, k * LANES : (k + 1) * LANES]
    arrive(so)
    whole_ref[...] = sum(b["small_all"][u] for u in range(TP))
    for u in range(TP):
        for k in range(7):
            table_ref[0:1, k * D + u * LANES : k * D + (u + 1) * LANES] = b["small_all"][
                u, 5:6, k * LANES : (k + 1) * LANES
            ]
    for p in range(2):
        arrive(hring[p])
        h = plus(xs[2 * core + p, x], b["ring_h"].at[p])
        st = tab[2 * core + p, x]
        r = st[:, HD + ROT : HD + ROT + 1]
        n = (x_ref[p].astype(F32) - st[:, ROT : ROT + 1]) * r
        inner = (
            h - jnp.mean(h, axis=1, keepdims=True) - n * jnp.mean(h * n, axis=1, keepdims=True)
        )
        dx_ref[p] = (g_ref[p].astype(F32) + r * inner).astype(BF)
    arrive(po)
    for u in range(TP):
        for m in range(3):
            pwg_ref[:, m * D + u * LANES : m * D + (u + 1) * LANES] = b["pg_all"][u, :, m * LANES : (m + 1) * LANES]
    for c in wire.copies:
        c.wait_send()


def finish_kernel(out, dx, pwg, owg, ewg, rwg, whole, table, *results):
    for ref, to in zip((out, dx, pwg, owg, ewg, rwg), results):
        to[...] = ref[...]
    index = lax.axis_index("dp") * 8 + lax.axis_index("ctx")
    v = pltpu.roll(whole[...], (D - 8 * index) % D, 1)
    for i in range(5):
        results[6 + i][...] = v[i : i + 1, :8]
    wide = jnp.broadcast_to(table[...], (8, 7 * D))
    v = pltpu.roll(wide[:, : 3 * D], (3 * D - 24 * index) % (3 * D), 1)
    results[11][...] = v[0:1, :24]
    v = pltpu.roll(wide[:, 3 * D :], (FF - 32 * index) % FF, 1)
    results[12][...] = v[0:1, :32]


def shards(
    inputs, positions, first_gain, first_shift, second_gain, second_shift, project_weight,
    project_bias, output_weight, output_bias, expand_weight, expand_bias, reduce_weight,
    reduce_bias, cotangent,
):
    inverse = 10000.0 ** (-(np.arange(ROT // 2, dtype=np.float32) * 2.0 / ROT))
    by_lane = np.zeros((2, HD), np.float32)
    by_lane[:, :ROT] = np.concatenate([inverse, inverse]).astype(np.float32)
    by_lane = by_lane.reshape(1, LANES)
    inside = np.arange(STRETCH, dtype=np.float64)[:, None] * by_lane
    line = lambda v: v.reshape(1, -1)
    shape = jax.ShapeDtypeStruct
    out, dx, pwg, owg, ewg, rwg, whole, table = pl.pallas_call(
        block_kernel,
        name="block",
        out_shape=(
            shape((2, PART, D), BF),
            shape((2, PART, D), BF),
            shape((OWN, 3 * D), F32),
            shape((OWN, D), F32),
            shape((OWN, FF), F32),
            shape((OWN, GROUPS, D), F32),
            shape((8, D), F32),
            shape((1, 7 * D), F32),
        ),
        in_specs=[VMEM] * 18,
        out_specs=(VMEM,) * 8,
        scratch_shapes=[pltpu.VMEM(*v) for v in SCRATCH.values()]
        + [pltpu.SemaphoreType.DMA((COPIES,)), pltpu.SemaphoreType.DMA((COPIES,))],
        compiler_params=pltpu.CompilerParams(
            collective_id=0, has_side_effects=True, vmem_limit_bytes=64 * 2**20
        ),
    )(
        inputs, cotangent, positions, jnp.asarray(by_lane),
        jnp.asarray(np.cos(inside).astype(np.float32)), jnp.asarray(np.sin(inside).astype(np.float32)),
        line(first_gain), line(first_shift), line(second_gain), line(second_shift),
        project_weight, line(project_bias), output_weight, line(output_bias),
        expand_weight, line(expand_bias), reduce_weight, line(reduce_bias),
    )
    results = pl.pallas_call(
        finish_kernel,
        name="finish",
        out_shape=[shape(v.shape, v.dtype) for v in (out, dx, pwg, owg, ewg, rwg)]
        + [shape((1, n), F32) for n in (8, 8, 8, 8, 8, 24, 32)],
        in_specs=[VMEM] * 8,
        out_specs=[VMEM] * 13,
    )(out, dx, pwg, owg, ewg, rwg, whole, table)
    out, dx, pwg, owg, ewg, rwg, *vectors = results
    a, c, d, e, f, g, h = (v.reshape(-1) for v in vectors)
    return out, dx, a, c, d, e, pwg, g, owg, f, ewg, h, rwg, f


def solution(mesh):
    rows = P(("dp", "ctx"), None)
    vector = P(("dp", "ctx"))
    tokens = P("dp", "ctx", None)
    deep = P(("dp", "ctx"), None, None)
    return jax.shard_map(
        shards,
        mesh=mesh,
        in_specs=(
            tokens, P("dp", None), P(), P(), P(), P(), rows, P(), rows, P(), rows, P(), deep, P(),
            tokens,
        ),
        out_specs=(
            tokens, tokens, vector, vector, vector, vector, rows, vector, rows, vector, rows,
            vector, deep, vector,
        ),
        check_vma=False,
    )
```

```python
import jax
import jax.numpy as jnp
import numpy as np
from jax import lax
from jax.experimental import pallas as pl
from jax.experimental.pallas import tpu as pltpu
from jax.sharding import PartitionSpec as P

D = 1024
HD = 64
ROT = 16
FF = 4096
GROUPS = 4
EPSILON = 1e-05

RING = 4
TP = 8
SEQ = 4
PART = 128
STRETCH = 64
HALF = RING * PART
FULL = 2 * HALF
OWN = 8
LANES = 128
QKV = 3 * LANES
HID = GROUPS * LANES
WIDE = QKV + HID
SCALE = HD ** (-0.5)
BLOCK = 256

MESH = pl.DeviceIdType.MESH
VMEM = pl.BlockSpec(memory_space=pltpu.VMEM)
BF = jnp.bfloat16
F32 = jnp.float32


def place():
    dp, ctx = lax.axis_index("dp"), lax.axis_index("ctx")
    return ctx % 4, (ctx // 4) * 2 + dp // 8, (dp // 2) % 4, dp % 2


def device(x, y, z, core):
    return {"dp": ((y % 2) * 4 + z) * 2 + core, "ctx": (y // 2) * 4 + x}


class Copy:
    def __init__(self, copy):
        self.copy, self.left, self.here = copy, False, False

    def wait_send(self):
        if not self.left:
            self.left = True
            self.copy.wait_send()

    def wait_recv(self):
        if not self.here:
            self.here = True
            self.copy.wait_recv()


class Wire:
    def __init__(self, send, recv):
        self.send, self.recv, self.copies = send, recv, []

    def push(self, src, dst, to):
        i = len(self.copies)
        copy = pltpu.make_async_remote_copy(
            src_ref=src,
            dst_ref=dst,
            send_sem=self.send.at[i],
            recv_sem=self.recv.at[i],
            device_id=to,
            device_id_type=MESH,
        )
        copy.start()
        self.copies.append(Copy(copy))
        return self.copies[-1]


def arrive(copies):
    for c in copies:
        c.wait_recv()


def row_owner(x, y, z, core):
    ylo = y % 2
    return device(ylo * 2 + z // 2, core * 2 + y // 2, (x + 3 + 2 * ylo) % 4, z % 2)


def row_source(x, y, z, core):
    ylo = x // 2
    return device((z + 1 + 2 * ylo) % 4, (y % 2) * 2 + ylo, (x % 2) * 2 + core, y // 2)


def row_block(x, y, z):
    return y, (z + 1 + 2 * (x // 2)) % 4


def fold(rows):
    return jnp.concatenate([rows[:, : D // 2], rows[:, D // 2 :]], axis=0).astype(BF)


def unfold(rows):
    return jnp.concatenate([rows[:OWN], rows[OWN:]], axis=1)


def mul(a, b, ca=1, cb=0):
    return lax.dot_general(a, b, (((ca,), (cb,)), ((), ())), preferred_element_type=F32)


def lane_of(rows):
    return lax.broadcasted_iota(jnp.int32, (rows, LANES), 1)


def turn(v, cosine, sine):
    low = lane_of(v.shape[0]) % HD < ROT // 2
    mate = jnp.where(low, pltpu.roll(v, LANES - ROT // 2, 1), pltpu.roll(v, ROT // 2, 1))
    return v * cosine + mate * sine


def column(row):
    r = lax.broadcasted_iota(jnp.int32, (PART, 1), 0)
    base = jnp.where(r < STRETCH, row[:, 0:1], row[:, STRETCH : STRETCH + 1])
    return base + (r % STRETCH).astype(F32)


def colsum(v):
    return jnp.sum(v, axis=0, keepdims=True)


SCRATCH = dict(
    pe_s=((TP, 2 * OWN, D // 2), BF),
    stage=((2, 4, 2 * OWN, D // 2), BF),
    wp=((2, 4, 2, 2, 4 * OWN, QKV), BF),
    we=((2, 4, 2, 2, 4 * OWN, HID), BF),
    wo_own=((2 * OWN, D // 2), BF),
    wr_f=((GROUPS, OWN, D), F32),
    wr_own=((GROUPS * OWN, D), BF),
    wos=((4, 4, 2 * OWN, D // 2), BF),
    wrs=((4, 4, GROUPS * OWN, D), BF),
    wo=((LANES, D), BF),
    wr=((HID, D), BF),
    xs=((SEQ, RING, PART, D), BF),
    gs=((SEQ, RING, PART, D), BF),
    ps=((2, 8, FULL), F32),
    first=((SEQ, RING, PART, D), BF),
    second=((SEQ, RING, PART, D), BF),
    tab=((SEQ, RING, PART, LANES), F32),
    qs=((SEQ, RING, PART, LANES), BF),
    kv=((2, SEQ, 2, RING, PART, LANES), BF),
    att=((SEQ, HALF, LANES), BF),
    hid=((SEQ, RING, PART, HID), BF),
    dexp=((SEQ, RING, PART, HID), BF),
    datt=((SEQ, RING, PART, LANES), BF),
    dkv_own=((SEQ, 2, LANES, HALF), F32),
    dkv_out=((SEQ, 2, LANES, HALF), BF),
    dkv_in=((SEQ, 2, LANES, HALF), BF),
    dproj=((SEQ, HALF, QKV), BF),
    ob=((2, 2, RING, PART, D), BF),
    half=((2, RING, PART, D), BF),
    via_o=((2, 2, PART // 2, D), BF),
    via_h=((2, 2, PART // 2, D), BF),
    ring_o=((2, 2, PART, D), BF),
    ring_h=((2, 2, PART, D), BF),
    small=((8, D), F32),
    small_in=((6, 8, D), F32),
    small_b=((8, D), F32),
    small_g=((8, D), F32),
    small_all=((TP, 8, D), F32),
    rg_a=((3, 4, 2 * OWN, D), BF),
    rg_b=((3, 4, 2 * OWN, D), BF),
    rg_m=((2, 4, 2 * OWN, D), BF),
    rg_n=((2, 3, 2 * OWN, D), BF),
    rg_f=((GROUPS * OWN, D), F32),
    rg_all=((GROUPS * OWN, D), F32),
    og_a=((3, 4, 2 * OWN, D // 2), BF),
    og_m=((4, 2 * OWN, D // 2), BF),
    og_n=((3, 2 * OWN, D // 2), BF),
    og_f=((OWN, D), F32),
    eg=((2, 4, 2, 2, 4 * OWN, HID), BF),
    eg_a=((3, 2, 2, 4 * OWN, HID), BF),
    eg_b=((3, 4, 4 * OWN, HID), BF),
    eg_m=((2, 2, 4 * OWN, HID), BF),
    eg_k=((4, 4 * OWN, HID), BF),
    eg_n=((2, 3, 4 * OWN, HID), BF),
    eg_f=((2, 4, OWN, HID), F32),
    eg_all=((TP, OWN, HID), F32),
    pg=((2, 4, 2, 2, 4 * OWN, QKV), BF),
    pg_a=((3, 2, 2, 4 * OWN, QKV), BF),
    pg_b=((3, 4, 4 * OWN, QKV), BF),
    pg_m=((2, 2, 4 * OWN, QKV), BF),
    pg_k=((4, 4 * OWN, QKV), BF),
    pg_n=((2, 3, 4 * OWN, QKV), BF),
    pg_f=((2, 4, OWN, QKV), F32),
    pg_all=((TP, OWN, QKV), F32),
)
COPIES = 192


def block_kernel(
    x_ref, g_ref, pos_ref, inv_ref, cos_in, sin_in, g1, s1, g2, s2, pw_ref, bp_ref, ow_ref, bo_ref, ew_ref, be_ref,
    rw_ref, br_ref,
    out_ref, dx_ref, pwg_ref, owg_ref, ewg_ref, rwg_ref, whole_ref, table_ref,
    *scratch,
):
    b = dict(zip(SCRATCH, scratch))
    send, recv = scratch[len(SCRATCH) :]
    xs, gs, ps, first, second, tab = (b[n] for n in ("xs", "gs", "ps", "first", "second", "tab"))
    wp, we, wos, wrs, wo, wr, kv = (b[n] for n in ("wp", "we", "wos", "wrs", "wo", "wr", "kv"))
    small = b["small"]
    x, y, z, core = place()
    me = (x, y, z, core)
    t = x * 2 + core
    ylo, yhi = y % 2, y // 2
    sib = device(x, y, z, 1 - core)
    xp = [device((x + d) % 4, y, z, core) for d in (1, 2, 3)]
    xq = [device((x + d) % 4, y, z, 1 - core) for d in (1, 2, 3)]
    yp = [device(x, (y + d) % 4, z, core) for d in (1, 2, 3)]
    zp = [device(x, y, (z + d) % 4, core) for d in (1, 2, 3)]
    mine = pl.ds(2 * core, 2)
    group = [(x, 1 - core, sib)]
    group += [((x + d) % 4, core, xp[d - 1]) for d in (1, 2, 3)]
    group += [((x + d) % 4, 1 - core, xq[d - 1]) for d in (1, 2, 3)]
    t128 = pl.multiple_of(t * LANES, LANES)

    senders = xp + [sib] + xq + yp + zp + [row_source(*me), row_owner(*me)]
    barrier = pltpu.get_barrier_semaphore()
    for other in senders:
        pl.semaphore_signal(barrier, inc=1, device_id=other, device_id_type=MESH)

    pw, ew = pw_ref[...].astype(F32), ew_ref[...].astype(F32)
    for u in range(TP):
        at = slice(u * LANES, (u + 1) * LANES)
        parts = [pw[:, m * D : (m + 1) * D][:, at] for m in range(3)]
        parts += [ew[:, k * D : (k + 1) * D][:, at] for k in range(GROUPS)]
        b["pe_s"][u] = fold(jnp.concatenate(parts + [jnp.zeros((OWN, LANES), F32)], axis=1))
    xs[mine, x] = x_ref[...]
    pl.semaphore_wait(barrier, len(senders))
    wire = Wire(send, recv)
    push = wire.push

    def to_neighbours(buf):
        a, c, both = buf.at[2 * core, x], buf.at[2 * core + 1, x], buf.at[mine, x]
        ahead = push(a, a, xp[0])
        back = push(c, c, xp[2])
        return [ahead, back, push(both, both, sib), push(c, c, xp[0]), push(a, a, xp[2])]

    step = [push(b["pe_s"].at[ux * 2 + uc], b["stage"].at[core, x], other) for ux, uc, other in group]
    b["stage"][core, x] = b["pe_s"][t]
    b["wo_own"][...] = fold(ow_ref[...].astype(F32))
    for i in range(OWN):
        b["wr_f"][:, i, :] = rw_ref[i].astype(F32)
    b["wr_own"][...] = b["wr_f"][...].reshape(GROUPS * OWN, D).astype(BF)
    by, bz = row_block(*me[:3])
    owner = row_owner(*me)
    oy, oz = core * 2 + yhi, x
    step_rows = [
        push(b["wo_own"], wos.at[oy, oz], owner),
        push(b["wr_own"], wrs.at[oy, oz], owner),
    ]
    xc = to_neighbours(xs)
    ps[core] = jnp.zeros((8, FULL), F32)
    ps[core, 0:2] = pos_ref[...].astype(F32)
    sp = push(ps.at[core], ps.at[core], sib)
    gs[mine, x] = g_ref[...]
    small[...] = jnp.zeros_like(small)
    tab[...] = jnp.zeros_like(tab)

    def keep_turn(s, j, v, turning):
        tab[s, j] = jnp.where((lane_of(PART) % HD < ROT) == turning, v, tab[s, j])

    def angles(v):
        lane, back = lane_of(v.shape[0]), pltpu.roll(v, HD, 1)
        turned = lane % HD < ROT
        cosine = jnp.where(turned, jnp.where(lane < HD, v, back), 1.0)
        return cosine, jnp.where(turned, jnp.where(lane < HD, back, v), 0.0)

    def layer_norm(s0, count, j):
        @pl.loop(0, count)
        def _(i):
            s = s0 + i
            v = xs[s, j].astype(F32)
            mean = jnp.mean(v, axis=1, keepdims=True)
            c = v - mean
            r = lax.rsqrt(jnp.mean(c * c, axis=1, keepdims=True) + EPSILON)
            n = c * r
            first[s, j] = (n * g1[...] + s1[...]).astype(BF)
            second[s, j] = (n * g2[...] + s2[...]).astype(BF)
            keep_turn(s, j, jnp.where(lane_of(PART) < HD, mean, r), False)

    def tables():
        firsts = []
        for s in range(SEQ):
            row = ps[s // 2, s % 2 : s % 2 + 1, pl.ds(pl.multiple_of(yhi * HALF, HALF), HALF)]
            firsts += [row[:, i * STRETCH : i * STRETCH + 1] for i in range(2 * RING)]
        angle = jnp.concatenate(firsts, axis=0) * inv_ref[...]
        cosine, sine = jnp.cos(angle), jnp.sin(angle)
        lane = lane_of(STRETCH)
        sign = jnp.where(lane % HD < ROT // 2, -1.0, 1.0)
        for s in range(SEQ):
            for j in range(RING):
                two = []
                for i in range(2):
                    n = (s * RING + j) * 2 + i
                    c, v = cosine[n : n + 1], sine[n : n + 1]
                    both = jnp.where(
                        lane < HD,
                        c * cos_in[...] - v * sin_in[...],
                        (v * cos_in[...] + c * sin_in[...]) * sign,
                    )
                    two.append(both)
                keep_turn(s, j, jnp.concatenate(two, axis=0), True)

    bias_p = jnp.concatenate([bp_ref[:, pl.ds(pl.multiple_of(m * D + t128, LANES), LANES)] for m in range(3)], axis=1)
    bias_e = jnp.concatenate(
        [be_ref[:, pl.ds(pl.multiple_of(k * D + t128, LANES), LANES)] for k in range(GROUPS)], axis=1
    )

    def project(j):
        p = mul(first[:, j].reshape(HALF, D), wp[...].reshape(D, QKV)) + bias_p
        c, s = angles(tab[:, j].reshape(HALF, LANES))
        shape = (SEQ, PART, LANES)
        b["qs"][:, j] = (turn(p[:, :LANES], c, s) * SCALE).astype(BF).reshape(shape)
        kv[0, :, 0, j] = turn(p[:, LANES : 2 * LANES], c, s).astype(BF).reshape(shape)
        kv[1, :, 0, j] = p[:, 2 * LANES :].astype(BF).reshape(shape)
        return push(kv.at[:, :, 0, j], kv.at[:, :, 1, j], yp[1])

    def expand(j):
        e = mul(second[:, j].reshape(HALF, D), we[...].reshape(D, HID)) + bias_e
        cdf = 0.5 * (1.0 + lax.erf(e * 0.5**0.5))
        b["hid"][:, j] = (e * cdf).astype(BF).reshape(SEQ, PART, HID)
        slope = cdf + e * (jnp.exp(-0.5 * e * e) * (2.0 * np.pi) ** -0.5)
        b["dexp"][:, j] = slope.astype(BF).reshape(SEQ, PART, HID)

    def across_y(buf):
        out = []
        for d in (0, 2, 1):
            v = buf.at[ylo, z, 0, yhi]
            out.append(push(v, v, yp[d]))
            v = buf.at[ylo, z, 1, yhi]
            out.append(push(v, v, zp[d]))
        return out

    def across_z(buf):
        out = []
        for d in (0, 2, 1):
            v = buf.at[:, z, 0]
            out.append(push(v, v, zp[d]))
            v = buf.at[ylo, :, 1, yhi]
            out.append(push(v, v, yp[d]))
        return out

    def across_y(buf):
        out = []
        for d in (0, 2, 1):
            v = buf.at[ylo, z, 0, yhi]
            out.append(push(v, v, yp[d]))
            v = buf.at[ylo, z, 1, yhi]
            out.append(push(v, v, zp[d]))
        return out

    def across_z(buf):
        out = []
        for d in (0, 2, 1):
            v = buf.at[:, z, 0]
            out.append(push(v, v, zp[d]))
            v = buf.at[ylo, :, 1, yhi]
            out.append(push(v, v, yp[d]))
        return out

    def along_y(v):
        return [push(v, v, yp[d]) for d in (0, 2, 1)]

    def near_z(v):
        return [push(v, v, zp[0]), push(v, v, zp[2])]

    def far_z(came, ahead, back):
        came[0].wait_recv()
        out = [push(ahead, ahead, zp[0])]
        came[1].wait_recv()
        return out + [push(back, back, zp[2])]

    layer_norm(2 * core, 2, x)
    xc[2].wait_recv()
    layer_norm(2 - 2 * core, 2, x)
    sp.wait_recv()
    tables()
    arrive(step)
    for c in range(2):
        v = [unfold(b["stage"][c, i].astype(F32)) for i in range(4)]
        v = jnp.concatenate(v, axis=0).astype(BF)
        wp[ylo, z, c, yhi] = v[:, :QKV]
        we[ylo, z, c, yhi] = v[:, QKV:WIDE]
    p1 = across_y(wp)
    e1 = along_y(we.at[ylo, z, :, yhi])
    arrive(step_rows)
    o1 = along_y(wos.at[by, bz])
    w1 = along_y(wrs.at[by, bz])
    arrive(p1)
    p2 = across_z(wp)
    top, low = pl.ds(0, 2 * OWN), pl.ds(2 * OWN, 2 * OWN)
    before, after, far = (x + 3) % 4, (x + 1) % 4, (x + 2) % 4

    def relay(buf, near):
        near[0].wait_recv()
        v = buf.at[2 * core, before]
        ahead = push(v, v, xp[0])
        near[1].wait_recv()
        v = buf.at[2 * core + 1, after]
        back = push(v, v, xp[2])
        return [ahead, back]

    def relay_core(buf, near):
        v, w = buf.at[mine, before], buf.at[mine, after]
        near[3].wait_recv()
        out = [push(v, v, sib)]
        near[4].wait_recv()
        return out + [push(w, w, sib)]

    def relay_far(buf, fars):
        fars[0].wait_recv()
        v = buf.at[2 * core, far]
        a = push(v, v, sib)
        fars[1].wait_recv()
        w = buf.at[2 * core + 1, far]
        return [a, push(w, w, sib)]

    xf = relay(xs, xc)
    xd = relay_core(xs, xc)
    gc = to_neighbours(gs)
    layer_norm(2 * core, 2, before)
    layer_norm(2 * core, 2, after)
    arrive(p2)
    kc = [project(x)]
    arrive(e1)
    e2 = near_z(we.at[:, z])
    arrive(o1)
    o2 = []
    for d in (0, 2, 1):
        v = wos.at[:, bz]
        o2.append(push(v, v, zp[d]))
    arrive(xd)
    layer_norm(2 - 2 * core, 2, before)
    kc.append(project(before))
    xfd = relay_far(xs, xf)
    layer_norm(2 - 2 * core, 2, after)
    kc.append(project(after))
    e3 = far_z(e2, we.at[:, (z + 3) % 4, 0], we.at[:, (z + 1) % 4, 1])
    arrive(w1)
    w2 = near_z(wrs.at[:, bz])
    layer_norm(2 * core, 2, far)
    arrive(xfd)
    layer_norm(2 - 2 * core, 2, far)
    kc.append(project(far))
    arrive(e3)
    expand(x)
    gf = relay(gs, gc)
    gd = relay_core(gs, gc)
    w3 = far_z(w2, wrs.at[:, (bz + 3) % 4, top], wrs.at[:, (bz + 1) % 4, low])
    expand(before)
    arrive(o2)
    for i in range(8):
        two = [unfold(wos[2 * i // 4, 2 * i % 4 + n].astype(F32)) for n in range(2)]
        wo[2 * i * OWN : 2 * (i + 1) * OWN] = jnp.concatenate(two, axis=0).astype(BF)
    expand(after)
    gfd = relay_far(gs, gf)
    expand(far)

    arrive(w3)
    wr_all = wrs[...].reshape(16, GROUPS, OWN, D).astype(F32)
    for k in range(GROUPS):
        wr[k * LANES : (k + 1) * LANES] = wr_all[:, k].reshape(LANES, D).astype(BF)

    small[4:5] = colsum(g_ref[...].astype(F32).reshape(2 * PART, D))

    def back_attention(j):
        g = gs[:, j].reshape(HALF, D)
        b["datt"][:, j] = mul(g, wo[...], 1, 1).astype(BF).reshape(SEQ, PART, LANES)

    def back_hidden(j):
        g = gs[:, j].reshape(HALF, D)
        d = mul(g, wr[...], 1, 1) * b["dexp"][:, j].reshape(HALF, HID).astype(F32)
        small[5:6, QKV:WIDE] += colsum(d)
        b["dexp"][:, j] = d.astype(BF).reshape(SEQ, PART, HID)

    gc[2].wait_recv()
    back_attention(x)
    back_hidden(x)
    arrive(gd)
    back_attention(before)
    back_attention(after)
    back_hidden(before)
    arrive(gfd)
    back_attention(far)
    for c in xc + xf + xd + xfd + step_rows + o1 + o2 + w1 + w2 + w3:
        c.wait_send()
    arrive(kc)

    def attend(s):
        k, v = kv[0, s].reshape(FULL, LANES), kv[1, s].reshape(FULL, LANES)
        row = ps[s // 2, pl.ds(s % 2, 1), pl.ds(pl.multiple_of(yhi * HALF, HALF), HALF)]
        other = ps[s // 2, pl.ds(s % 2, 1), pl.ds(pl.multiple_of((1 - yhi) * HALF, HALF), HALF)]
        keys_at = jnp.concatenate([row, other], axis=1)
        lane = lane_of(BLOCK)
        zero = jnp.zeros((BLOCK, LANES), BF)
        v_one = [jnp.where(lane_of(FULL) // HD == h, v, jnp.ones_like(v)) for h in range(2)]
        dk = dv = None
        for i in range(HALF // BLOCK):
            few = slice(i * BLOCK // PART, (i + 1) * BLOCK // PART)
            at_rows = slice(i * BLOCK, (i + 1) * BLOCK)
            q, do = b["qs"][s, few].reshape(BLOCK, LANES), b["datt"][s, few].reshape(BLOCK, LANES)
            at = jnp.concatenate(
                [column(row[:, j * PART : (j + 1) * PART]) for j in range(few.start, few.stop)], axis=0
            )
            allowed = keys_at <= at
            out = jnp.zeros((BLOCK, LANES), F32)
            dq = jnp.zeros((BLOCK, LANES), F32)
            for h in range(2):
                m = lane // HD == h
                qh = jnp.where(m, q, zero)
                score = jnp.where(allowed, mul(qh, k, 1, 1), -1e30)
                raised = jnp.exp(score - jnp.max(score, axis=1, keepdims=True)).astype(BF)
                oh = mul(raised, v_one[h])
                inverse = jnp.where(m, 1.0 / pltpu.roll(oh, HD, 1), 0.0)
                oh = oh * inverse
                out = out + oh
                share = do.astype(F32) * inverse
                delta = jnp.sum(share * oh, axis=1, keepdims=True)
                share = share.astype(BF)
                ds = (raised.astype(F32) * (mul(share, v, 1, 1) - delta)).astype(BF)
                dq = jnp.where(m, mul(ds, k), dq)
                dkh, dvh = mul(qh, ds, 0, 0), mul(share, raised, 0, 0)
                dk, dv = (dkh, dvh) if dk is None else (dk + dkh, dv + dvh)
            b["att"][s, at_rows] = out.astype(BF)
            cosine, sine = angles(tab[s, few].reshape(BLOCK, LANES))
            dq = turn(dq * SCALE, cosine, -sine)
            small[5:6, :LANES] += colsum(dq)
            b["dproj"][s, at_rows, :LANES] = dq.astype(BF)
        for n, v in enumerate((dk, dv)):
            b["dkv_own"][s, n] = v[:, :HALF]
            b["dkv_out"][s, n] = v[:, HALF:].astype(BF)

    def branches(p, c):
        s = 2 * c + p
        v = mul(b["att"][s], wo[...]) + mul(b["hid"][s].reshape(HALF, HID), wr[...])
        b["ob"][p, c] = v.astype(BF).reshape(RING, PART, D)

    def combine(ref, at, half, p):
        @pl.loop(0, RING)
        def _(i):
            ref[(*at, i)] = (ref[(*at, i)].astype(F32) + half[p, i].astype(F32)).astype(BF)

    def far_block(ref, at, via, p):
        halves = ref.at[(*at, far, pl.ds(0, PART // 2))], ref.at[(*at, far, pl.ds(PART // 2, PART // 2))]
        return [push(v, via.at[p, i], xp[2 * i]) for i, v in enumerate(halves)]

    def near_blocks(ref, at, via, ring, p, came):
        out = []
        for i, to in enumerate((after, before)):
            came[i].wait_recv()
            where = (*at, to, pl.ds(i * PART // 2, PART // 2))
            ref[where] = (ref[where].astype(F32) + via[p, i].astype(F32)).astype(BF)
            v = ref.at[(*at, to)]
            out.append(push(v, ring.at[p, i], xp[2 * i]))
        return out

    rows = SEQ * HALF

    def weight_grad(into, back_ref, to):
        for i in range(4):
            v = into[..., i * 2 * LANES : (i + 1) * 2 * LANES].reshape(rows, 2 * LANES)
            back = back_ref[...].reshape(rows, back_ref.shape[-1])
            e = mul(v, back, 0, 0).astype(BF).reshape(2, 2, 2, 4 * OWN, back.shape[1])
            to[i // 2, 2 * (i % 2) : 2 * (i % 2) + 2] = e

    def plus(first_term, inbox):
        v = first_term.astype(F32)
        for i in range(inbox.shape[0]):
            v = v + inbox[i].astype(F32)
        return v

    def reduce_1(name):
        g = b[name]
        out = []
        for d in (1, 3, 2):
            out.append(push(g.at[:, (z + d) % 4, 0], b[name + "_a"].at[d - 1], zp[d - 1]))
            to = (y + d) % 4
            out.append(push(g.at[to % 2, :, 1, to // 2], b[name + "_b"].at[d - 1], yp[d - 1]))
        return out

    def reduce_2(name, came):
        arrive(came)
        g, m, k, n = b[name], b[name + "_m"], b[name + "_k"], b[name + "_n"]
        m[...] = plus(g[:, z, 0], b[name + "_a"]).astype(BF)
        k[...] = plus(g[ylo, :, 1, yhi], b[name + "_b"]).astype(BF)
        out = []
        for d in (1, 3, 2):
            to = (y + d) % 4
            out.append(push(m.at[to % 2, to // 2], n.at[0, d - 1], yp[d - 1]))
            out.append(push(k.at[(z + d) % 4], n.at[1, d - 1], zp[d - 1]))
        return out

    def to_owners(name, came):
        arrive(came)
        f, whole, n = b[name + "_f"], b[name + "_all"], b[name + "_n"]
        width = f.shape[-1]
        f[0] = plus(b[name + "_m"][ylo, yhi], n.at[0]).reshape(4, OWN, width)
        f[1] = plus(b[name + "_k"][z], n.at[1]).reshape(4, OWN, width)
        whole[t] = f[core, x]
        return [push(f.at[uc, ux], whole.at[t], other) for ux, uc, other in group]

    theirs, ours = 1 - core, core

    def pair(f, p):
        @pl.loop(0, 2)
        def _(c):
            f(2 * ((c + theirs) % 2) + p)

    ob, half = b["ob"], b["half"]
    pair(attend, 0)
    dc = [push(b["dkv_out"].at[s], b["dkv_in"].at[s], yp[1]) for s in (0, 2)]
    branches(0, theirs)
    oc = [push(ob.at[0, theirs], half.at[0], sib)]
    branches(0, ours)
    back_hidden(after)
    back_hidden(far)

    for k in range(2):
        two = slice(2 * k * LANES, 2 * (k + 1) * LANES)
        r = mul(b["hid"][..., two].reshape(rows, 2 * LANES), gs[...].reshape(rows, D), 0, 0)
        r = r.reshape(2, 16, OWN, D)
        for j in range(16):
            wrs[j // 4, j % 4, 2 * k * OWN : 2 * (k + 1) * OWN] = r[:, j].reshape(2 * OWN, D).astype(BF)
    rc = []
    for d in (1, 3, 2):
        rc.append(push(wrs.at[:, (bz + d) % 4, top], b["rg_a"].at[d - 1], zp[d - 1]))
        rc.append(push(wrs.at[(y + d) % 4, :, low], b["rg_b"].at[d - 1], yp[d - 1]))
    arrive(oc)
    combine(ob, (0, core), half, 0)
    ofar = [far_block(ob, (0, core), b["via_o"], 0)]

    def return_keys(s):
        return push(b["dkv_out"].at[s], b["dkv_in"].at[s], yp[1])

    attend(2 * theirs + 1)
    dc.append(return_keys(2 * theirs + 1))
    oring = [near_blocks(ob, (0, core), b["via_o"], b["ring_o"], 0, ofar[0])]
    attend(2 * ours + 1)
    dc.append(return_keys(2 * ours + 1))
    branches(1, theirs)
    oc.append(push(ob.at[1, theirs], half.at[1], sib))
    branches(1, ours)

    o = mul(b["att"][...].reshape(rows, LANES), gs[...].reshape(rows, D), 0, 0)
    for j in range(16):
        wos[j // 4, j % 4] = fold(o[j * OWN : (j + 1) * OWN])
    arrive(rc)
    b["rg_m"][0] = plus(wrs[:, bz, top], b["rg_a"]).astype(BF)
    b["rg_m"][1] = plus(wrs[y, :, low], b["rg_b"]).astype(BF)
    r2 = []
    for d in (1, 3, 2):
        r2.append(push(b["rg_m"].at[0, (y + d) % 4], b["rg_n"].at[0, d - 1], yp[d - 1]))
        r2.append(push(b["rg_m"].at[1, (bz + d) % 4], b["rg_n"].at[1, d - 1], zp[d - 1]))
    og1 = [push(wos.at[:, (bz + d) % 4], b["og_a"].at[d - 1], zp[d - 1]) for d in (1, 3, 2)]
    arrive(oc)
    combine(ob, (1, core), half, 1)
    ofar.append(far_block(ob, (1, core), b["via_o"], 1))

    def finish_keys(s):
        for n in range(2):
            v = (b["dkv_own"][s, n] + b["dkv_in"][s, n].astype(F32)).T
            if n == 0:
                cosine, sine = angles(tab[s].reshape(HALF, LANES))
                v = turn(v, cosine, -sine)
            small[5:6, (n + 1) * LANES : (n + 2) * LANES] += colsum(v)
            b["dproj"][s, :, (n + 1) * LANES : (n + 2) * LANES] = v.astype(BF)

    def inward(s, i):
        two = pl.ds(2 * i, 2)
        some = 2 * PART
        da = mul(
            b["dproj"][s, pl.ds(pl.multiple_of(i * some, some), some)], wp[...].reshape(D, QKV), 1, 1
        )
        db = mul(b["dexp"][s, two].reshape(some, HID), we[...].reshape(D, HID), 1, 1)
        st = tab[s, two].reshape(some, LANES)
        n = (xs[s, two].reshape(some, D).astype(F32) - st[:, ROT : ROT + 1]) * st[:, HD + ROT : HD + ROT + 1]
        small[0:1] += colsum(da * n)
        small[1:2] += colsum(da)
        small[2:3] += colsum(db * n)
        small[3:4] += colsum(db)
        xs[s, two] = (da * g1[...] + db * g2[...]).astype(BF).reshape(2, PART, D)

    def inward_all(s):
        @pl.loop(0, 2)
        def _(i):
            inward(s, i)

    def swap_half(i):
        two = pl.ds(2 * i, 2)
        return push(xs.at[2 * theirs + 1, two], half.at[1, two], sib)

    def combine_half(i):
        two = pl.ds(2 * i, 2)
        s = 2 * core + 1
        xs[s, two] = (xs[s, two].astype(F32) + half[1, two].astype(F32)).astype(BF)

    arrive(dc[:2])
    pair(finish_keys, 0)
    inward_all(2 * theirs)
    hc = [push(xs.at[2 * theirs], half.at[0], sib)]
    oring.append(near_blocks(ob, (1, core), b["via_o"], b["ring_o"], 1, ofar[1]))
    inward_all(2 * ours)
    arrive(hc)
    combine(xs, (2 * core,), half, 0)
    hfar = [far_block(xs, (2 * core,), b["via_h"], 0)]
    weight_grad(second, b["dexp"], b["eg"])
    ec = reduce_1("eg")
    arrive(og1)
    b["og_m"][...] = plus(wos[:, bz], b["og_a"]).astype(BF)
    og2 = [push(b["og_m"].at[(y + d) % 4], b["og_n"].at[d - 1], yp[d - 1]) for d in (1, 3, 2)]

    arrive(dc[2:])
    pair(finish_keys, 1)
    hring = [near_blocks(xs, (2 * core,), b["via_h"], b["ring_h"], 0, hfar[0])]
    weight_grad(first, b["dproj"], b["pg"])
    pc = reduce_1("pg")
    arrive(r2)
    b["rg_f"][top] = plus(b["rg_m"][0, y], b["rg_n"].at[0])
    b["rg_f"][low] = plus(b["rg_m"][1, bz], b["rg_n"].at[1])
    source = row_source(*me)
    back = [push(b["rg_f"], b["rg_all"], source)]

    one = far // 2
    inward(2 * theirs + 1, one)
    hc = [swap_half(one)]
    inward(2 * ours + 1, one)
    arrive(hc)
    combine_half(one)
    hfar.append(far_block(xs, (2 * core + 1,), b["via_h"], 1))
    inward(2 * theirs + 1, 1 - one)
    hc = [swap_half(1 - one)]
    ec = reduce_2("eg", ec)
    inward(2 * ours + 1, 1 - one)
    sz = [push(small, b["small_in"].at[d - 1], zp[d - 1]) for d in (1, 2, 3)]
    arrive(hc)
    combine_half(1 - one)
    hring.append(near_blocks(xs, (2 * core + 1,), b["via_h"], b["ring_h"], 1, hfar[1]))

    pc = reduce_2("pg", pc)
    eo = to_owners("eg", ec)
    arrive(sz)
    b["small_b"][...] = plus(small[...], b["small_in"].at[pl.ds(0, 3)])
    sy = [push(b["small_b"], b["small_in"].at[2 + d], yp[d - 1]) for d in (1, 2, 3)]
    arrive(og2)
    b["og_f"][...] = unfold(plus(b["og_m"][y], b["og_n"]))
    back.append(push(b["og_f"], owg_ref, source))
    po = to_owners("pg", pc)
    arrive(sy)
    b["small_g"][...] = plus(b["small_b"][...], b["small_in"].at[pl.ds(3, 3)])
    b["small_all"][t] = b["small_g"][...]
    so = [push(b["small_g"], b["small_all"].at[t], other) for _, _, other in group]
    for p in range(2):
        arrive(oring[p])
        v = plus(ob[p, core, x], b["ring_o"].at[p])
        out_ref[p] = (x_ref[p].astype(F32) + v + bo_ref[...] + br_ref[...]).astype(BF)

    def input_grad(p):
        arrive(hring[p])
        h = plus(xs[2 * core + p, x], b["ring_h"].at[p])
        st = tab[2 * core + p, x]
        r = st[:, HD + ROT : HD + ROT + 1]
        n = (x_ref[p].astype(F32) - st[:, ROT : ROT + 1]) * r
        inner = (
            h - jnp.mean(h, axis=1, keepdims=True) - n * jnp.mean(h * n, axis=1, keepdims=True)
        )
        dx_ref[p] = (g_ref[p].astype(F32) + r * inner).astype(BF)

    input_grad(0)
    arrive(back)
    r = b["rg_all"][...].reshape(GROUPS, OWN, D)
    for k in range(GROUPS):
        rwg_ref[:, k, :] = r[k]
    arrive(eo)
    for u in range(TP):
        for k in range(GROUPS):
            ewg_ref[:, k * D + u * LANES : k * D + (u + 1) * LANES] = b["eg_all"][u, :, k * LANES : (k + 1) * LANES]
    arrive(po)
    for u in range(TP):
        for m in range(3):
            pwg_ref[:, m * D + u * LANES : m * D + (u + 1) * LANES] = b["pg_all"][u, :, m * LANES : (m + 1) * LANES]
    arrive(so)
    whole_ref[...] = sum(b["small_all"][u] for u in range(TP))
    for u in range(TP):
        for k in range(7):
            table_ref[0:1, k * D + u * LANES : k * D + (u + 1) * LANES] = b["small_all"][
                u, 5:6, k * LANES : (k + 1) * LANES
            ]
    input_grad(1)
    for c in wire.copies:
        c.wait_send()


def finish_kernel(out, dx, pwg, owg, ewg, rwg, whole, table, *results):
    for ref, to in zip((out, dx, pwg, owg, ewg, rwg), results):
        to[...] = ref[...]
    index = lax.axis_index("dp") * 8 + lax.axis_index("ctx")
    v = pltpu.roll(whole[...], (D - 8 * index) % D, 1)
    for i in range(5):
        results[6 + i][...] = v[i : i + 1, :8]
    wide = jnp.broadcast_to(table[...], (8, 7 * D))
    v = pltpu.roll(wide[:, : 3 * D], (3 * D - 24 * index) % (3 * D), 1)
    results[11][...] = v[0:1, :24]
    v = pltpu.roll(wide[:, 3 * D :], (FF - 32 * index) % FF, 1)
    results[12][...] = v[0:1, :32]


def shards(
    inputs, positions, first_gain, first_shift, second_gain, second_shift, project_weight,
    project_bias, output_weight, output_bias, expand_weight, expand_bias, reduce_weight,
    reduce_bias, cotangent,
):
    inverse = 10000.0 ** (-(np.arange(ROT // 2, dtype=np.float32) * 2.0 / ROT))
    by_lane = np.zeros((2, HD), np.float32)
    by_lane[:, :ROT] = np.concatenate([inverse, inverse]).astype(np.float32)
    by_lane = by_lane.reshape(1, LANES)
    inside = np.arange(STRETCH, dtype=np.float64)[:, None] * by_lane
    line = lambda v: v.reshape(1, -1)
    shape = jax.ShapeDtypeStruct
    out, dx, pwg, owg, ewg, rwg, whole, table = pl.pallas_call(
        block_kernel,
        name="block",
        out_shape=(
            shape((2, PART, D), BF),
            shape((2, PART, D), BF),
            shape((OWN, 3 * D), F32),
            shape((OWN, D), F32),
            shape((OWN, FF), F32),
            shape((OWN, GROUPS, D), F32),
            shape((8, D), F32),
            shape((1, 7 * D), F32),
        ),
        in_specs=[VMEM] * 18,
        out_specs=(VMEM,) * 8,
        scratch_shapes=[pltpu.VMEM(*v) for v in SCRATCH.values()]
        + [pltpu.SemaphoreType.DMA((COPIES,)), pltpu.SemaphoreType.DMA((COPIES,))],
        compiler_params=pltpu.CompilerParams(
            collective_id=0, has_side_effects=True, vmem_limit_bytes=64 * 2**20
        ),
    )(
        inputs, cotangent, positions, jnp.asarray(by_lane),
        jnp.asarray(np.cos(inside).astype(np.float32)), jnp.asarray(np.sin(inside).astype(np.float32)),
        line(first_gain), line(first_shift), line(second_gain), line(second_shift),
        project_weight, line(project_bias), output_weight, line(output_bias),
        expand_weight, line(expand_bias), reduce_weight, line(reduce_bias),
    )
    results = pl.pallas_call(
        finish_kernel,
        name="finish",
        out_shape=[shape(v.shape, v.dtype) for v in (out, dx, pwg, owg, ewg, rwg)]
        + [shape((1, n), F32) for n in (8, 8, 8, 8, 8, 24, 32)],
        in_specs=[VMEM] * 8,
        out_specs=[VMEM] * 13,
    )(out, dx, pwg, owg, ewg, rwg, whole, table)
    out, dx, pwg, owg, ewg, rwg, *vectors = results
    a, c, d, e, f, g, h = (v.reshape(-1) for v in vectors)
    return out, dx, a, c, d, e, pwg, g, owg, f, ewg, h, rwg, f


def solution(mesh):
    rows = P(("dp", "ctx"), None)
    vector = P(("dp", "ctx"))
    tokens = P("dp", "ctx", None)
    deep = P(("dp", "ctx"), None, None)
    return jax.shard_map(
        shards,
        mesh=mesh,
        in_specs=(
            tokens, P("dp", None), P(), P(), P(), P(), rows, P(), rows, P(), rows, P(), deep, P(),
            tokens,
        ),
        out_specs=(
            tokens, tokens, vector, vector, vector, vector, rows, vector, rows, vector, rows,
            vector, deep, vector,
        ),
        check_vma=False,
    )
```

```python
import jax
import jax.numpy as jnp
import numpy as np
from jax import lax
from jax.experimental import pallas as pl
from jax.experimental.pallas import tpu as pltpu
from jax.sharding import PartitionSpec as P

D = 1024
HD = 64
ROT = 16
FF = 4096
GROUPS = 4
EPSILON = 1e-05

RING = 4
TP = 8
SEQ = 4
PART = 128
STRETCH = 64
HALF = RING * PART
FULL = 2 * HALF
OWN = 8
LANES = 128
QKV = 3 * LANES
HID = GROUPS * LANES
WIDE = QKV + HID
SCALE = HD ** (-0.5)
BLOCK = 256

MESH = pl.DeviceIdType.MESH
VMEM = pl.BlockSpec(memory_space=pltpu.VMEM)
BF = jnp.bfloat16
F32 = jnp.float32


def place():
    dp, ctx = lax.axis_index("dp"), lax.axis_index("ctx")
    return ctx % 4, (ctx // 4) * 2 + dp // 8, (dp // 2) % 4, dp % 2


def device(x, y, z, core):
    return {"dp": ((y % 2) * 4 + z) * 2 + core, "ctx": (y // 2) * 4 + x}


class Copy:
    def __init__(self, copy):
        self.copy, self.left, self.here = copy, False, False

    def wait_send(self):
        if not self.left:
            self.left = True
            self.copy.wait_send()

    def wait_recv(self):
        if not self.here:
            self.here = True
            self.copy.wait_recv()


class Wire:
    def __init__(self, send, recv):
        self.send, self.recv, self.copies = send, recv, []

    def push(self, src, dst, to):
        i = len(self.copies)
        copy = pltpu.make_async_remote_copy(
            src_ref=src,
            dst_ref=dst,
            send_sem=self.send.at[i],
            recv_sem=self.recv.at[i],
            device_id=to,
            device_id_type=MESH,
        )
        copy.start()
        self.copies.append(Copy(copy))
        return self.copies[-1]


def arrive(copies):
    for c in copies:
        c.wait_recv()


def row_owner(x, y, z, core):
    ylo = y % 2
    return device(ylo * 2 + z // 2, core * 2 + y // 2, (x + 3 + 2 * ylo) % 4, z % 2)


def row_source(x, y, z, core):
    ylo = x // 2
    return device((z + 1 + 2 * ylo) % 4, (y % 2) * 2 + ylo, (x % 2) * 2 + core, y // 2)


def row_block(x, y, z):
    return y, (z + 1 + 2 * (x // 2)) % 4


def fold(rows):
    return jnp.concatenate([rows[:, : D // 2], rows[:, D // 2 :]], axis=0).astype(BF)


def unfold(rows):
    return jnp.concatenate([rows[:OWN], rows[OWN:]], axis=1)


def mul(a, b, ca=1, cb=0):
    return lax.dot_general(a, b, (((ca,), (cb,)), ((), ())), preferred_element_type=F32)


def lane_of(rows):
    return lax.broadcasted_iota(jnp.int32, (rows, LANES), 1)


def turn(v, cosine, sine):
    low = lane_of(v.shape[0]) % HD < ROT // 2
    mate = jnp.where(low, pltpu.roll(v, LANES - ROT // 2, 1), pltpu.roll(v, ROT // 2, 1))
    return v * cosine + mate * sine


def column(row):
    r = lax.broadcasted_iota(jnp.int32, (PART, 1), 0)
    base = jnp.where(r < STRETCH, row[:, 0:1], row[:, STRETCH : STRETCH + 1])
    return base + (r % STRETCH).astype(F32)


def colsum(v):
    return jnp.sum(v, axis=0, keepdims=True)


SCRATCH = dict(
    pe_s=((TP, 2 * OWN, D // 2), BF),
    stage=((2, 4, 2 * OWN, D // 2), BF),
    wp=((2, 4, 2, 2, 4 * OWN, QKV), BF),
    we=((2, 4, 2, 2, 4 * OWN, HID), BF),
    wo_own=((2 * OWN, D // 2), BF),
    wr_f=((GROUPS, OWN, D), F32),
    wr_own=((GROUPS * OWN, D), BF),
    wos=((4, 4, 2 * OWN, D // 2), BF),
    wrs=((4, 4, GROUPS * OWN, D), BF),
    wo=((LANES, D), BF),
    wr=((HID, D), BF),
    xs=((SEQ, RING, PART, D), BF),
    gs=((SEQ, RING, PART, D), BF),
    ps=((2, 8, FULL), F32),
    first=((SEQ, RING, PART, D), BF),
    second=((SEQ, RING, PART, D), BF),
    tab=((SEQ, RING, PART, LANES), F32),
    qs=((SEQ, RING, PART, LANES), BF),
    kv=((2, SEQ, 2, RING, PART, LANES), BF),
    att=((SEQ, HALF, LANES), BF),
    hid=((SEQ, RING, PART, HID), BF),
    dexp=((SEQ, RING, PART, HID), BF),
    datt=((SEQ, RING, PART, LANES), BF),
    dkv_own=((SEQ, 2, LANES, HALF), F32),
    dkv_out=((SEQ, 2, LANES, HALF), BF),
    dkv_in=((SEQ, 2, LANES, HALF), BF),
    dproj=((SEQ, HALF, QKV), BF),
    ob=((2, 2, RING, PART, D), BF),
    half=((2, RING, PART, D), BF),
    via_o=((2, 2, PART // 2, D), BF),
    via_h=((2, 2, PART // 2, D), BF),
    ring_o=((2, 2, PART, D), BF),
    ring_h=((2, 2, PART, D), BF),
    small=((8, D), F32),
    small_in=((6, 8, D), F32),
    small_b=((8, D), F32),
    small_g=((8, D), F32),
    small_all=((TP, 8, D), F32),
    rg_a=((3, 4, 2 * OWN, D), BF),
    rg_b=((3, 4, 2 * OWN, D), BF),
    rg_m=((2, 4, 2 * OWN, D), BF),
    rg_n=((2, 3, 2 * OWN, D), BF),
    rg_f=((GROUPS * OWN, D), F32),
    rg_all=((GROUPS * OWN, D), F32),
    og_a=((3, 4, 2 * OWN, D // 2), BF),
    og_m=((4, 2 * OWN, D // 2), BF),
    og_n=((3, 2 * OWN, D // 2), BF),
    og_f=((OWN, D), F32),
    eg=((2, 4, 2, 2, 4 * OWN, HID), BF),
    eg_a=((3, 2, 2, 4 * OWN, HID), BF),
    eg_b=((3, 4, 4 * OWN, HID), BF),
    eg_m=((2, 2, 4 * OWN, HID), BF),
    eg_k=((4, 4 * OWN, HID), BF),
    eg_n=((2, 3, 4 * OWN, HID), BF),
    eg_f=((2, 4, OWN, HID), F32),
    eg_all=((TP, OWN, HID), F32),
    pg=((2, 4, 2, 2, 4 * OWN, QKV), BF),
    pg_a=((3, 2, 2, 4 * OWN, QKV), BF),
    pg_b=((3, 4, 4 * OWN, QKV), BF),
    pg_m=((2, 2, 4 * OWN, QKV), BF),
    pg_k=((4, 4 * OWN, QKV), BF),
    pg_n=((2, 3, 4 * OWN, QKV), BF),
    pg_f=((2, 4, OWN, QKV), F32),
    pg_all=((TP, OWN, QKV), F32),
)
COPIES = 192


def block_kernel(
    x_ref, g_ref, pos_ref, inv_ref, cos_in, sin_in, g1, s1, g2, s2, pw_ref, bp_ref, ow_ref, bo_ref, ew_ref, be_ref,
    rw_ref, br_ref,
    out_ref, dx_ref, pwg_ref, owg_ref, ewg_ref, rwg_ref, whole_ref, table_ref,
    *scratch,
):
    b = dict(zip(SCRATCH, scratch))
    send, recv = scratch[len(SCRATCH) :]
    xs, gs, ps, first, second, tab = (b[n] for n in ("xs", "gs", "ps", "first", "second", "tab"))
    wp, we, wos, wrs, wo, wr, kv = (b[n] for n in ("wp", "we", "wos", "wrs", "wo", "wr", "kv"))
    small = b["small"]
    x, y, z, core = place()
    me = (x, y, z, core)
    t = x * 2 + core
    ylo, yhi = y % 2, y // 2
    sib = device(x, y, z, 1 - core)
    xp = [device((x + d) % 4, y, z, core) for d in (1, 2, 3)]
    xq = [device((x + d) % 4, y, z, 1 - core) for d in (1, 2, 3)]
    yp = [device(x, (y + d) % 4, z, core) for d in (1, 2, 3)]
    zp = [device(x, y, (z + d) % 4, core) for d in (1, 2, 3)]
    mine = pl.ds(2 * core, 2)
    group = [(x, 1 - core, sib)]
    group += [((x + d) % 4, core, xp[d - 1]) for d in (1, 2, 3)]
    group += [((x + d) % 4, 1 - core, xq[d - 1]) for d in (1, 2, 3)]
    t128 = pl.multiple_of(t * LANES, LANES)

    senders = xp + [sib] + xq + yp + zp + [row_source(*me), row_owner(*me)]
    barrier = pltpu.get_barrier_semaphore()
    for other in senders:
        pl.semaphore_signal(barrier, inc=1, device_id=other, device_id_type=MESH)

    pw, ew = pw_ref[...].astype(F32), ew_ref[...].astype(F32)
    for u in range(TP):
        at = slice(u * LANES, (u + 1) * LANES)
        parts = [pw[:, m * D : (m + 1) * D][:, at] for m in range(3)]
        parts += [ew[:, k * D : (k + 1) * D][:, at] for k in range(GROUPS)]
        b["pe_s"][u] = fold(jnp.concatenate(parts + [jnp.zeros((OWN, LANES), F32)], axis=1))
    xs[mine, x] = x_ref[...]
    pl.semaphore_wait(barrier, len(senders))
    wire = Wire(send, recv)
    push = wire.push

    def to_neighbours(buf):
        a, c, both = buf.at[2 * core, x], buf.at[2 * core + 1, x], buf.at[mine, x]
        ahead = push(a, a, xp[0])
        back = push(c, c, xp[2])
        return [ahead, back, push(both, both, sib), push(c, c, xp[0]), push(a, a, xp[2])]

    step = [push(b["pe_s"].at[ux * 2 + uc], b["stage"].at[core, x], other) for ux, uc, other in group]
    b["stage"][core, x] = b["pe_s"][t]
    b["wo_own"][...] = fold(ow_ref[...].astype(F32))
    for i in range(OWN):
        b["wr_f"][:, i, :] = rw_ref[i].astype(F32)
    b["wr_own"][...] = b["wr_f"][...].reshape(GROUPS * OWN, D).astype(BF)
    by, bz = row_block(*me[:3])
    owner = row_owner(*me)
    oy, oz = core * 2 + yhi, x
    step_rows = [
        push(b["wo_own"], wos.at[oy, oz], owner),
        push(b["wr_own"], wrs.at[oy, oz], owner),
    ]
    xc = to_neighbours(xs)
    ps[core] = jnp.zeros((8, FULL), F32)
    ps[core, 0:2] = pos_ref[...].astype(F32)
    sp = push(ps.at[core], ps.at[core], sib)
    gs[mine, x] = g_ref[...]
    small[...] = jnp.zeros_like(small)
    tab[...] = jnp.zeros_like(tab)

    def keep_turn(s, j, v, turning):
        tab[s, j] = jnp.where((lane_of(PART) % HD < ROT) == turning, v, tab[s, j])

    def angles(v):
        lane, back = lane_of(v.shape[0]), pltpu.roll(v, HD, 1)
        turned = lane % HD < ROT
        cosine = jnp.where(turned, jnp.where(lane < HD, v, back), 1.0)
        return cosine, jnp.where(turned, jnp.where(lane < HD, back, v), 0.0)

    def layer_norm(s0, count, j):
        @pl.loop(0, count)
        def _(i):
            s = s0 + i
            v = xs[s, j].astype(F32)
            mean = jnp.mean(v, axis=1, keepdims=True)
            c = v - mean
            r = lax.rsqrt(jnp.mean(c * c, axis=1, keepdims=True) + EPSILON)
            n = c * r
            first[s, j] = (n * g1[...] + s1[...]).astype(BF)
            second[s, j] = (n * g2[...] + s2[...]).astype(BF)
            keep_turn(s, j, jnp.where(lane_of(PART) < HD, mean, r), False)

    def tables():
        firsts = []
        for s in range(SEQ):
            row = ps[s // 2, s % 2 : s % 2 + 1, pl.ds(pl.multiple_of(yhi * HALF, HALF), HALF)]
            firsts += [row[:, i * STRETCH : i * STRETCH + 1] for i in range(2 * RING)]
        angle = jnp.concatenate(firsts, axis=0) * inv_ref[...]
        cosine, sine = jnp.cos(angle), jnp.sin(angle)
        lane = lane_of(STRETCH)
        sign = jnp.where(lane % HD < ROT // 2, -1.0, 1.0)
        for s in range(SEQ):
            for j in range(RING):
                two = []
                for i in range(2):
                    n = (s * RING + j) * 2 + i
                    c, v = cosine[n : n + 1], sine[n : n + 1]
                    both = jnp.where(
                        lane < HD,
                        c * cos_in[...] - v * sin_in[...],
                        (v * cos_in[...] + c * sin_in[...]) * sign,
                    )
                    two.append(both)
                keep_turn(s, j, jnp.concatenate(two, axis=0), True)

    bias_p = jnp.concatenate([bp_ref[:, pl.ds(pl.multiple_of(m * D + t128, LANES), LANES)] for m in range(3)], axis=1)
    bias_e = jnp.concatenate(
        [be_ref[:, pl.ds(pl.multiple_of(k * D + t128, LANES), LANES)] for k in range(GROUPS)], axis=1
    )

    def project(j):
        p = mul(first[:, j].reshape(HALF, D), wp[...].reshape(D, QKV)) + bias_p
        c, s = angles(tab[:, j].reshape(HALF, LANES))
        shape = (SEQ, PART, LANES)
        b["qs"][:, j] = (turn(p[:, :LANES], c, s) * SCALE).astype(BF).reshape(shape)
        kv[0, :, 0, j] = turn(p[:, LANES : 2 * LANES], c, s).astype(BF).reshape(shape)
        kv[1, :, 0, j] = p[:, 2 * LANES :].astype(BF).reshape(shape)
        return push(kv.at[:, :, 0, j], kv.at[:, :, 1, j], yp[1])

    def expand(j):
        e = mul(second[:, j].reshape(HALF, D), we[...].reshape(D, HID)) + bias_e
        cdf = 0.5 * (1.0 + lax.erf(e * 0.5**0.5))
        b["hid"][:, j] = (e * cdf).astype(BF).reshape(SEQ, PART, HID)
        slope = cdf + e * (jnp.exp(-0.5 * e * e) * (2.0 * np.pi) ** -0.5)
        b["dexp"][:, j] = slope.astype(BF).reshape(SEQ, PART, HID)

    def across_y(buf):
        out = []
        for d in (0, 2, 1):
            v = buf.at[ylo, z, 0, yhi]
            out.append(push(v, v, yp[d]))
            v = buf.at[ylo, z, 1, yhi]
            out.append(push(v, v, zp[d]))
        return out

    def across_z(buf):
        out = []
        for d in (0, 2, 1):
            v = buf.at[:, z, 0]
            out.append(push(v, v, zp[d]))
            v = buf.at[ylo, :, 1, yhi]
            out.append(push(v, v, yp[d]))
        return out

    def across_y(buf):
        out = []
        for d in (0, 2, 1):
            v = buf.at[ylo, z, 0, yhi]
            out.append(push(v, v, yp[d]))
            v = buf.at[ylo, z, 1, yhi]
            out.append(push(v, v, zp[d]))
        return out

    def across_z(buf):
        out = []
        for d in (0, 2, 1):
            v = buf.at[:, z, 0]
            out.append(push(v, v, zp[d]))
            v = buf.at[ylo, :, 1, yhi]
            out.append(push(v, v, yp[d]))
        return out

    def along_y(v):
        return [push(v, v, yp[d]) for d in (0, 2, 1)]

    def near_z(v):
        return [push(v, v, zp[0]), push(v, v, zp[2])]

    def far_z(came, ahead, back):
        came[0].wait_recv()
        out = [push(ahead, ahead, zp[0])]
        came[1].wait_recv()
        return out + [push(back, back, zp[2])]

    layer_norm(2 * core, 2, x)
    xc[2].wait_recv()
    layer_norm(2 - 2 * core, 2, x)
    sp.wait_recv()
    tables()
    arrive(step)
    for c in range(2):
        v = [unfold(b["stage"][c, i].astype(F32)) for i in range(4)]
        v = jnp.concatenate(v, axis=0).astype(BF)
        wp[ylo, z, c, yhi] = v[:, :QKV]
        we[ylo, z, c, yhi] = v[:, QKV:WIDE]
    p1 = across_y(wp)
    e1 = along_y(we.at[ylo, z, :, yhi])
    arrive(step_rows)
    o1 = along_y(wos.at[by, bz])
    w1 = along_y(wrs.at[by, bz])
    arrive(p1)
    p2 = across_z(wp)
    top, low = pl.ds(0, 2 * OWN), pl.ds(2 * OWN, 2 * OWN)
    before, after, far = (x + 3) % 4, (x + 1) % 4, (x + 2) % 4

    def relay(buf, near):
        near[0].wait_recv()
        v = buf.at[2 * core, before]
        ahead = push(v, v, xp[0])
        near[1].wait_recv()
        v = buf.at[2 * core + 1, after]
        back = push(v, v, xp[2])
        return [ahead, back]

    def relay_core(buf, near):
        v, w = buf.at[mine, before], buf.at[mine, after]
        near[3].wait_recv()
        out = [push(v, v, sib)]
        near[4].wait_recv()
        return out + [push(w, w, sib)]

    def relay_far(buf, fars):
        fars[0].wait_recv()
        v = buf.at[2 * core, far]
        a = push(v, v, sib)
        fars[1].wait_recv()
        w = buf.at[2 * core + 1, far]
        return [a, push(w, w, sib)]

    xf = relay(xs, xc)
    xd = relay_core(xs, xc)
    gc = to_neighbours(gs)
    layer_norm(2 * core, 2, before)
    layer_norm(2 * core, 2, after)
    arrive(p2)
    kc = [project(x)]
    arrive(e1)
    e2 = near_z(we.at[:, z])
    arrive(o1)
    o2 = []
    for d in (0, 2, 1):
        v = wos.at[:, bz]
        o2.append(push(v, v, zp[d]))
    arrive(xd)
    layer_norm(2 - 2 * core, 2, before)
    kc.append(project(before))
    xfd = relay_far(xs, xf)
    layer_norm(2 - 2 * core, 2, after)
    kc.append(project(after))
    e3 = far_z(e2, we.at[:, (z + 3) % 4, 0], we.at[:, (z + 1) % 4, 1])
    arrive(w1)
    w2 = near_z(wrs.at[:, bz])
    layer_norm(2 * core, 2, far)
    arrive(xfd)
    layer_norm(2 - 2 * core, 2, far)
    kc.append(project(far))
    arrive(e3)
    expand(x)
    gf = relay(gs, gc)
    gd = relay_core(gs, gc)
    w3 = far_z(w2, wrs.at[:, (bz + 3) % 4, top], wrs.at[:, (bz + 1) % 4, low])
    expand(before)
    arrive(o2)
    for i in range(8):
        two = [unfold(wos[2 * i // 4, 2 * i % 4 + n].astype(F32)) for n in range(2)]
        wo[2 * i * OWN : 2 * (i + 1) * OWN] = jnp.concatenate(two, axis=0).astype(BF)
    expand(after)
    gfd = relay_far(gs, gf)
    expand(far)

    arrive(w3)
    wr_all = wrs[...].reshape(16, GROUPS, OWN, D).astype(F32)
    for k in range(GROUPS):
        wr[k * LANES : (k + 1) * LANES] = wr_all[:, k].reshape(LANES, D).astype(BF)

    small[4:5] = colsum(g_ref[...].astype(F32).reshape(2 * PART, D))

    def back_attention(j):
        g = gs[:, j].reshape(HALF, D)
        b["datt"][:, j] = mul(g, wo[...], 1, 1).astype(BF).reshape(SEQ, PART, LANES)

    def back_hidden(j):
        g = gs[:, j].reshape(HALF, D)
        d = mul(g, wr[...], 1, 1) * b["dexp"][:, j].reshape(HALF, HID).astype(F32)
        small[5:6, QKV:WIDE] += colsum(d)
        b["dexp"][:, j] = d.astype(BF).reshape(SEQ, PART, HID)

    gc[2].wait_recv()
    back_attention(x)
    back_hidden(x)
    arrive(gd)
    back_attention(before)
    back_attention(after)
    back_hidden(before)
    arrive(gfd)
    back_attention(far)
    for c in xc + xf + xd + xfd + step_rows + o1 + o2 + w1 + w2 + w3:
        c.wait_send()
    arrive(kc)

    def attend(s):
        k, v = kv[0, s].reshape(FULL, LANES), kv[1, s].reshape(FULL, LANES)
        row = ps[s // 2, pl.ds(s % 2, 1), pl.ds(pl.multiple_of(yhi * HALF, HALF), HALF)]
        other = ps[s // 2, pl.ds(s % 2, 1), pl.ds(pl.multiple_of((1 - yhi) * HALF, HALF), HALF)]
        keys_at = jnp.concatenate([row, other], axis=1)
        lane = lane_of(BLOCK)
        zero = jnp.zeros((BLOCK, LANES), BF)
        v_one = [jnp.where(lane_of(FULL) // HD == h, v, jnp.ones_like(v)) for h in range(2)]
        dk = dv = None
        for i in range(HALF // BLOCK):
            few = slice(i * BLOCK // PART, (i + 1) * BLOCK // PART)
            at_rows = slice(i * BLOCK, (i + 1) * BLOCK)
            q, do = b["qs"][s, few].reshape(BLOCK, LANES), b["datt"][s, few].reshape(BLOCK, LANES)
            at = jnp.concatenate(
                [column(row[:, j * PART : (j + 1) * PART]) for j in range(few.start, few.stop)], axis=0
            )
            allowed = keys_at <= at
            out = jnp.zeros((BLOCK, LANES), F32)
            dq = jnp.zeros((BLOCK, LANES), F32)
            for h in range(2):
                m = lane // HD == h
                qh = jnp.where(m, q, zero)
                score = jnp.where(allowed, mul(qh, k, 1, 1), -1e30)
                raised = jnp.exp(score - jnp.max(score, axis=1, keepdims=True)).astype(BF)
                oh = mul(raised, v_one[h])
                inverse = jnp.where(m, 1.0 / pltpu.roll(oh, HD, 1), 0.0)
                oh = oh * inverse
                out = out + oh
                share = do.astype(F32) * inverse
                delta = jnp.sum(share * oh, axis=1, keepdims=True)
                share = share.astype(BF)
                ds = (raised.astype(F32) * (mul(share, v, 1, 1) - delta)).astype(BF)
                dq = jnp.where(m, mul(ds, k), dq)
                dkh, dvh = mul(qh, ds, 0, 0), mul(share, raised, 0, 0)
                dk, dv = (dkh, dvh) if dk is None else (dk + dkh, dv + dvh)
            b["att"][s, at_rows] = out.astype(BF)
            cosine, sine = angles(tab[s, few].reshape(BLOCK, LANES))
            dq = turn(dq * SCALE, cosine, -sine)
            small[5:6, :LANES] += colsum(dq)
            b["dproj"][s, at_rows, :LANES] = dq.astype(BF)
        for n, v in enumerate((dk, dv)):
            b["dkv_own"][s, n] = v[:, :HALF]
            b["dkv_out"][s, n] = v[:, HALF:].astype(BF)

    def branches(p, c):
        s = 2 * c + p
        v = mul(b["att"][s], wo[...]) + mul(b["hid"][s].reshape(HALF, HID), wr[...])
        b["ob"][p, c] = v.astype(BF).reshape(RING, PART, D)

    def combine(ref, at, half, p):
        @pl.loop(0, RING)
        def _(i):
            ref[(*at, i)] = (ref[(*at, i)].astype(F32) + half[p, i].astype(F32)).astype(BF)

    def far_block(ref, at, via, p):
        halves = ref.at[(*at, far, pl.ds(0, PART // 2))], ref.at[(*at, far, pl.ds(PART // 2, PART // 2))]
        return [push(v, via.at[p, i], xp[2 * i]) for i, v in enumerate(halves)]

    def near_blocks(ref, at, via, ring, p, came):
        out = []
        for i, to in enumerate((after, before)):
            came[i].wait_recv()
            where = (*at, to, pl.ds(i * PART // 2, PART // 2))
            ref[where] = (ref[where].astype(F32) + via[p, i].astype(F32)).astype(BF)
            v = ref.at[(*at, to)]
            out.append(push(v, ring.at[p, i], xp[2 * i]))
        return out

    rows = SEQ * HALF

    def weight_grad(into, back_ref, to):
        for i in range(4):
            v = into[..., i * 2 * LANES : (i + 1) * 2 * LANES].reshape(rows, 2 * LANES)
            back = back_ref[...].reshape(rows, back_ref.shape[-1])
            e = mul(v, back, 0, 0).astype(BF).reshape(2, 2, 2, 4 * OWN, back.shape[1])
            to[i // 2, 2 * (i % 2) : 2 * (i % 2) + 2] = e

    def plus(first_term, inbox):
        v = first_term.astype(F32)
        for i in range(inbox.shape[0]):
            v = v + inbox[i].astype(F32)
        return v

    def reduce_1(name):
        g = b[name]
        out = []
        for d in (1, 3, 2):
            out.append(push(g.at[:, (z + d) % 4, 0], b[name + "_a"].at[d - 1], zp[d - 1]))
            to = (y + d) % 4
            out.append(push(g.at[to % 2, :, 1, to // 2], b[name + "_b"].at[d - 1], yp[d - 1]))
        return out

    def reduce_2(name, came):
        arrive(came)
        g, m, k, n = b[name], b[name + "_m"], b[name + "_k"], b[name + "_n"]
        m[...] = plus(g[:, z, 0], b[name + "_a"]).astype(BF)
        k[...] = plus(g[ylo, :, 1, yhi], b[name + "_b"]).astype(BF)
        out = []
        for d in (1, 3, 2):
            to = (y + d) % 4
            out.append(push(m.at[to % 2, to // 2], n.at[0, d - 1], yp[d - 1]))
            out.append(push(k.at[(z + d) % 4], n.at[1, d - 1], zp[d - 1]))
        return out

    def to_owners(name, came):
        arrive(came)
        f, whole, n = b[name + "_f"], b[name + "_all"], b[name + "_n"]
        width = f.shape[-1]
        f[0] = plus(b[name + "_m"][ylo, yhi], n.at[0]).reshape(4, OWN, width)
        f[1] = plus(b[name + "_k"][z], n.at[1]).reshape(4, OWN, width)
        whole[t] = f[core, x]
        return [push(f.at[uc, ux], whole.at[t], other) for ux, uc, other in group]

    theirs, ours = 1 - core, core

    def pair(f, p):
        @pl.loop(0, 2)
        def _(c):
            f(2 * ((c + theirs) % 2) + p)

    ob, half = b["ob"], b["half"]
    pair(attend, 0)
    dc = [push(b["dkv_out"].at[s], b["dkv_in"].at[s], yp[1]) for s in (0, 2)]
    branches(0, theirs)
    oc = [push(ob.at[0, theirs], half.at[0], sib)]
    branches(0, ours)
    back_hidden(after)
    back_hidden(far)

    for k in range(2):
        two = slice(2 * k * LANES, 2 * (k + 1) * LANES)
        r = mul(b["hid"][..., two].reshape(rows, 2 * LANES), gs[...].reshape(rows, D), 0, 0)
        r = r.reshape(2, 16, OWN, D)
        for j in range(16):
            wrs[j // 4, j % 4, 2 * k * OWN : 2 * (k + 1) * OWN] = r[:, j].reshape(2 * OWN, D).astype(BF)
    rc = []
    for d in (1, 3, 2):
        rc.append(push(wrs.at[:, (bz + d) % 4, top], b["rg_a"].at[d - 1], zp[d - 1]))
        rc.append(push(wrs.at[(y + d) % 4, :, low], b["rg_b"].at[d - 1], yp[d - 1]))
    arrive(oc)
    combine(ob, (0, core), half, 0)
    ofar = [far_block(ob, (0, core), b["via_o"], 0)]

    def return_keys(s):
        return push(b["dkv_out"].at[s], b["dkv_in"].at[s], yp[1])

    attend(2 * theirs + 1)
    dc.append(return_keys(2 * theirs + 1))
    oring = [near_blocks(ob, (0, core), b["via_o"], b["ring_o"], 0, ofar[0])]
    attend(2 * ours + 1)
    dc.append(return_keys(2 * ours + 1))
    branches(1, theirs)
    oc.append(push(ob.at[1, theirs], half.at[1], sib))
    branches(1, ours)

    o = mul(b["att"][...].reshape(rows, LANES), gs[...].reshape(rows, D), 0, 0)
    for j in range(16):
        wos[j // 4, j % 4] = fold(o[j * OWN : (j + 1) * OWN])
    arrive(rc)
    b["rg_m"][0] = plus(wrs[:, bz, top], b["rg_a"]).astype(BF)
    b["rg_m"][1] = plus(wrs[y, :, low], b["rg_b"]).astype(BF)
    r2 = []
    for d in (1, 3, 2):
        r2.append(push(b["rg_m"].at[0, (y + d) % 4], b["rg_n"].at[0, d - 1], yp[d - 1]))
        r2.append(push(b["rg_m"].at[1, (bz + d) % 4], b["rg_n"].at[1, d - 1], zp[d - 1]))
    og1 = [push(wos.at[:, (bz + d) % 4], b["og_a"].at[d - 1], zp[d - 1]) for d in (1, 3, 2)]
    arrive(oc)
    combine(ob, (1, core), half, 1)
    ofar.append(far_block(ob, (1, core), b["via_o"], 1))

    def finish_keys(s):
        for n in range(2):
            v = (b["dkv_own"][s, n] + b["dkv_in"][s, n].astype(F32)).T
            if n == 0:
                cosine, sine = angles(tab[s].reshape(HALF, LANES))
                v = turn(v, cosine, -sine)
            small[5:6, (n + 1) * LANES : (n + 2) * LANES] += colsum(v)
            b["dproj"][s, :, (n + 1) * LANES : (n + 2) * LANES] = v.astype(BF)

    def inward(s, i):
        two = pl.ds(2 * i, 2)
        some = 2 * PART
        da = mul(
            b["dproj"][s, pl.ds(pl.multiple_of(i * some, some), some)], wp[...].reshape(D, QKV), 1, 1
        )
        db = mul(b["dexp"][s, two].reshape(some, HID), we[...].reshape(D, HID), 1, 1)
        st = tab[s, two].reshape(some, LANES)
        n = (xs[s, two].reshape(some, D).astype(F32) - st[:, ROT : ROT + 1]) * st[:, HD + ROT : HD + ROT + 1]
        small[0:1] += colsum(da * n)
        small[1:2] += colsum(da)
        small[2:3] += colsum(db * n)
        small[3:4] += colsum(db)
        xs[s, two] = (da * g1[...] + db * g2[...]).astype(BF).reshape(2, PART, D)

    def inward_all(s):
        @pl.loop(0, 2)
        def _(i):
            inward(s, i)

    def swap_half(i):
        two = pl.ds(2 * i, 2)
        return push(xs.at[2 * theirs + 1, two], half.at[1, two], sib)

    def combine_half(i):
        two = pl.ds(2 * i, 2)
        s = 2 * core + 1
        xs[s, two] = (xs[s, two].astype(F32) + half[1, two].astype(F32)).astype(BF)

    arrive(dc[:2])
    pair(finish_keys, 0)
    inward_all(2 * theirs)
    hc = [push(xs.at[2 * theirs], half.at[0], sib)]
    oring.append(near_blocks(ob, (1, core), b["via_o"], b["ring_o"], 1, ofar[1]))
    inward_all(2 * ours)
    arrive(hc)
    combine(xs, (2 * core,), half, 0)
    hfar = [far_block(xs, (2 * core,), b["via_h"], 0)]
    weight_grad(second, b["dexp"], b["eg"])
    ec = reduce_1("eg")
    arrive(og1)
    b["og_m"][...] = plus(wos[:, bz], b["og_a"]).astype(BF)
    og2 = [push(b["og_m"].at[(y + d) % 4], b["og_n"].at[d - 1], yp[d - 1]) for d in (1, 3, 2)]

    arrive(dc[2:])
    pair(finish_keys, 1)
    hring = [near_blocks(xs, (2 * core,), b["via_h"], b["ring_h"], 0, hfar[0])]
    weight_grad(first, b["dproj"], b["pg"])
    pc = reduce_1("pg")
    arrive(r2)
    b["rg_f"][top] = plus(b["rg_m"][0, y], b["rg_n"].at[0])
    b["rg_f"][low] = plus(b["rg_m"][1, bz], b["rg_n"].at[1])
    source = row_source(*me)
    back = [push(b["rg_f"], b["rg_all"], source)]

    one = far // 2
    inward(2 * theirs + 1, one)
    hc = [swap_half(one)]
    inward(2 * ours + 1, one)
    arrive(hc)
    combine_half(one)
    hfar.append(far_block(xs, (2 * core + 1,), b["via_h"], 1))
    inward(2 * theirs + 1, 1 - one)
    hc = [swap_half(1 - one)]
    ec = reduce_2("eg", ec)
    inward(2 * ours + 1, 1 - one)
    sz = [push(small, b["small_in"].at[d - 1], zp[d - 1]) for d in (1, 2, 3)]
    arrive(hc)
    combine_half(1 - one)
    hring.append(near_blocks(xs, (2 * core + 1,), b["via_h"], b["ring_h"], 1, hfar[1]))

    pc = reduce_2("pg", pc)
    eo = to_owners("eg", ec)
    arrive(sz)
    b["small_b"][...] = plus(small[...], b["small_in"].at[pl.ds(0, 3)])
    sy = [push(b["small_b"], b["small_in"].at[2 + d], yp[d - 1]) for d in (1, 2, 3)]
    arrive(og2)
    b["og_f"][...] = unfold(plus(b["og_m"][y], b["og_n"]))
    back.append(push(b["og_f"], owg_ref, source))
    po = to_owners("pg", pc)
    arrive(sy)
    b["small_g"][...] = plus(b["small_b"][...], b["small_in"].at[pl.ds(3, 3)])
    b["small_all"][t] = b["small_g"][...]
    so = [push(b["small_g"], b["small_all"].at[t], other) for _, _, other in group]
    for p in range(2):
        arrive(oring[p])
        v = plus(ob[p, core, x], b["ring_o"].at[p])
        out_ref[p] = (x_ref[p].astype(F32) + v + bo_ref[...] + br_ref[...]).astype(BF)

    def input_grad(p):
        arrive(hring[p])
        h = plus(xs[2 * core + p, x], b["ring_h"].at[p])
        st = tab[2 * core + p, x]
        r = st[:, HD + ROT : HD + ROT + 1]
        n = (x_ref[p].astype(F32) - st[:, ROT : ROT + 1]) * r
        inner = (
            h - jnp.mean(h, axis=1, keepdims=True) - n * jnp.mean(h * n, axis=1, keepdims=True)
        )
        dx_ref[p] = (g_ref[p].astype(F32) + r * inner).astype(BF)

    input_grad(0)
    arrive(back)
    r = b["rg_all"][...].reshape(GROUPS, OWN, D)
    for k in range(GROUPS):
        rwg_ref[:, k, :] = r[k]
    arrive(eo)
    for u in range(TP):
        for k in range(GROUPS):
            ewg_ref[:, k * D + u * LANES : k * D + (u + 1) * LANES] = b["eg_all"][u, :, k * LANES : (k + 1) * LANES]
    arrive(po)
    for u in range(TP):
        for m in range(3):
            pwg_ref[:, m * D + u * LANES : m * D + (u + 1) * LANES] = b["pg_all"][u, :, m * LANES : (m + 1) * LANES]
    arrive(so)
    whole_ref[...] = sum(b["small_all"][u] for u in range(TP))
    for u in range(TP):
        for k in range(7):
            table_ref[0:1, k * D + u * LANES : k * D + (u + 1) * LANES] = b["small_all"][
                u, 5:6, k * LANES : (k + 1) * LANES
            ]
    input_grad(1)
    for c in wire.copies:
        c.wait_send()


def shards(
    inputs, positions, first_gain, first_shift, second_gain, second_shift, project_weight,
    project_bias, output_weight, output_bias, expand_weight, expand_bias, reduce_weight,
    reduce_bias, cotangent,
):
    inverse = 10000.0 ** (-(np.arange(ROT // 2, dtype=np.float32) * 2.0 / ROT))
    by_lane = np.zeros((2, HD), np.float32)
    by_lane[:, :ROT] = np.concatenate([inverse, inverse]).astype(np.float32)
    by_lane = by_lane.reshape(1, LANES)
    inside = np.arange(STRETCH, dtype=np.float64)[:, None] * by_lane
    line = lambda v: v.reshape(1, -1)
    shape = jax.ShapeDtypeStruct
    out, dx, pwg, owg, ewg, rwg, whole, table = pl.pallas_call(
        block_kernel,
        name="block",
        out_shape=(
            shape((2, PART, D), BF),
            shape((2, PART, D), BF),
            shape((OWN, 3 * D), F32),
            shape((OWN, D), F32),
            shape((OWN, FF), F32),
            shape((OWN, GROUPS, D), F32),
            shape((8, D), F32),
            shape((1, 7 * D), F32),
        ),
        in_specs=[VMEM] * 18,
        out_specs=(VMEM,) * 8,
        scratch_shapes=[pltpu.VMEM(*v) for v in SCRATCH.values()]
        + [pltpu.SemaphoreType.DMA((COPIES,)), pltpu.SemaphoreType.DMA((COPIES,))],
        compiler_params=pltpu.CompilerParams(
            collective_id=0, has_side_effects=True, vmem_limit_bytes=64 * 2**20
        ),
    )(
        inputs, cotangent, positions, jnp.asarray(by_lane),
        jnp.asarray(np.cos(inside).astype(np.float32)), jnp.asarray(np.sin(inside).astype(np.float32)),
        line(first_gain), line(first_shift), line(second_gain), line(second_shift),
        project_weight, line(project_bias), output_weight, line(output_bias),
        expand_weight, line(expand_bias), reduce_weight, line(reduce_bias),
    )
    index = lax.axis_index("dp") * 8 + lax.axis_index("ctx")
    vec = lax.dynamic_slice_in_dim(whole, index * 8, 8, 1)
    bpg = lax.dynamic_slice_in_dim(table[0, : 3 * D], index * 24, 24, 0)
    beg = lax.dynamic_slice_in_dim(table[0, 3 * D :], index * 32, 32, 0)
    return (
        out, dx, vec[0], vec[1], vec[2], vec[3], pwg, bpg, owg, vec[4], ewg, beg, rwg, vec[4],
    )


def solution(mesh):
    rows = P(("dp", "ctx"), None)
    vector = P(("dp", "ctx"))
    tokens = P("dp", "ctx", None)
    deep = P(("dp", "ctx"), None, None)
    return jax.shard_map(
        shards,
        mesh=mesh,
        in_specs=(
            tokens, P("dp", None), P(), P(), P(), P(), rows, P(), rows, P(), rows, P(), deep, P(),
            tokens,
        ),
        out_specs=(
            tokens, tokens, vector, vector, vector, vector, rows, vector, rows, vector, rows,
            vector, deep, vector,
        ),
        check_vma=False,
    )
```
